32 devices in a mesh: row: 4 (over x, core), col: 8 (over z, y).
Axes of the slice: x: 2, y: 2, z: 4, core: 2. Of those that a mesh axis runs over, the one named last changes fastest.
Arguments:
- geometry: float32 [4, 49152], P(None, ('row', 'col')), may hold values from -1 to 1, as said below
- charges: bfloat16 [32, 49152], P(None, ('row', 'col')), may hold values from -6 to 6
- near_index: int32 [384, 128], P(('row', 'col')), may hold values from 0 to 4607
- near_count: int32 [384], P(('row', 'col')), may hold values from 1 to 128
- near_weight: bfloat16 [384, 128, 128], P(('row', 'col')), may hold values from -0.5 to 0.5
- conductor: int32 [49152], P(('row', 'col')), may hold values from 0 to 31
Outputs:
- potential: float32 [32, 49152], P(None, ('row', 'col'))
- conductor_totals: float32 [32, 32], replicated
The draws below stay inside these ranges and needn't reach their ends.
Inputs may be any that keep to these rules, and one draw needn't show every extreme that they name: `geometry`: rows 0 to 2 are coordinates in [-1, 1]; row 3 is a panel size in [0.05, 0.2].
All inputs are finite; a program needn't handle non-finite values.
Results may differ from the reference program's by a relative error of at most 0.0044.
Values may be sent and summed in bfloat16 or wider, within the bound.
No kernel may reach another device: no remote copies, remote signals or barrier semaphores. Data moves between devices by JAX's collectives and lax.ppermute only.
A program may use at most 64 MiB of HBM per device.

```python
import jax
import jax.numpy as jnp
from jax import lax

BLOCK = 1536
RHS = 32
ROUNDS = 8
GROUP = 128
NEAR = 128
PANELS = 49152
GROUPS = 384


def draw_geometry(key, part):
    place_key = jax.random.fold_in(key, 11)
    size_key = jax.random.fold_in(key, 12)
    coords = jax.random.uniform(place_key, (3, PANELS), jnp.float32, -1.0, 1.0)
    sizes = jnp.exp(jax.random.uniform(size_key, (1, PANELS), jnp.float32, jnp.log(0.05), jnp.log(0.2)))
    return jnp.concatenate([coords, sizes], axis=0).astype(jnp.float32)


def place_ends(drawn, key, least, top_value):
    place = [jax.random.randint(jax.random.fold_in(key, axis), (), 0, length) for axis, length in enumerate(drawn.shape)]
    main_axis = drawn.shape.index(max(drawn.shape))
    next_to = place[:main_axis] + [(place[main_axis] + 1) % drawn.shape[main_axis]] + place[main_axis + 1:]
    return drawn.at[tuple(place)].set(least).at[tuple(next_to)].set(top_value)


def level_of(stream_key, extent, split, smallest, high):
    def one(dim, blocks):
        steps = jax.random.uniform(jax.random.fold_in(jax.random.fold_in(stream_key, 6), dim), (blocks,), jnp.float32, smallest / len(split), high / len(split))
        return jnp.repeat(jnp.exp(steps), extent[dim] // blocks).reshape((-1,) + (1,) * (len(extent) - dim - 1))

    loudness = one(*split[0])
    for cut in split[1:]:
        loudness = loudness * one(*cut)
    return loudness


def bell_draw(rng, extent, deviation, limit, pieces=(), kind=jnp.bfloat16):
    values = deviation * jax.random.normal(rng, extent, jnp.float32)
    if pieces:
        values = values * level_of(rng, extent, pieces, -0.22, 0.18)
    return jnp.clip(values, -limit, limit).astype(kind)


def setup_inputs(seed: int = 0) -> dict:
    key_list = jax.random.split(jax.random.key(seed), 7)
    geometry = draw_geometry(jax.random.fold_in(key_list[6], 71), 0)
    charges = bell_draw(key_list[1], (RHS, PANELS), 1.0, 6.0, ((1, 32),))
    near_index = place_ends(jax.random.randint(key_list[2], (GROUPS, NEAR), 0, 3 * BLOCK), jax.random.fold_in(key_list[2], 1), 0, (3 * BLOCK) - 1).astype(jnp.int32)
    near_count = place_ends(jax.random.randint(key_list[3], (GROUPS,), 1, NEAR + 1), jax.random.fold_in(key_list[3], 1), 1, NEAR).astype(jnp.int32)
    near_weight = bell_draw(key_list[4], (GROUPS, GROUP, NEAR), NEAR ** -0.5, 0.5, ((0, 32),))
    conductor = place_ends(jax.random.randint(key_list[5], (PANELS,), 0, RHS), jax.random.fold_in(key_list[5], 1), 0, RHS - 1).astype(jnp.int32)
    return {"geometry": geometry, "charges": charges, "near_index": near_index, "near_count": near_count, "near_weight": near_weight, "conductor": conductor}


def kernel_tile(rows, cols):
    delta_x = rows[0][:, None] - cols[0][None, :]
    delta_y = rows[1][:, None] - cols[1][None, :]
    delta_z = rows[2][:, None] - cols[2][None, :]
    spread = rows[3][:, None] * rows[3][:, None] + cols[3][None, :] * cols[3][None, :]
    squared = delta_x * delta_x + delta_y * delta_y + delta_z * delta_z + spread
    return lax.rsqrt(squared).astype(jnp.bfloat16)

def reference(geometry, charges, near_index, near_count, near_weight, conductor):
    blocks = PANELS // BLOCK
    stride = blocks // (2 * ROUNDS)
    offsets = [1 + k * stride for k in range(ROUNDS)]
    groups_dev = BLOCK // GROUP
    area = geometry[3] * geometry[3]
    weighted = (charges.astype(jnp.float32) * area[None, :]).astype(jnp.bfloat16)

    def piece(array, block):
        return lax.dynamic_slice_in_dim(array, (block * BLOCK).astype(jnp.int32), BLOCK, 1)

    def visit(field, block):
        own_geo = piece(geometry, block)
        own_w = piece(weighted, block)
        tile = kernel_tile(own_geo, own_geo)
        forward = lax.dot_general(own_w, tile, (((1,), (1,)), ((), ())), preferred_element_type=jnp.float32)
        for offset in offsets:
            other = ((block - offset) % blocks).astype(jnp.int32)
            tile = kernel_tile(own_geo, piece(geometry, other))
            forward = forward + lax.dot_general(piece(weighted, other), tile, (((1,), (1,)), ((), ())), preferred_element_type=jnp.float32)
            back = jnp.dot(own_w, tile, preferred_element_type=jnp.float32).astype(jnp.bfloat16).astype(jnp.float32)
            start = (other * BLOCK).astype(jnp.int32)
            current = lax.dynamic_slice_in_dim(field, start, BLOCK, 1)
            field = lax.dynamic_update_slice_in_dim(field, current + back, start, 1)
        lower = ((block - 1) % blocks).astype(jnp.int32)
        upper = ((block + 1) % blocks).astype(jnp.int32)
        extended = jnp.concatenate([piece(charges, lower), piece(charges, block), piece(charges, upper)], axis=1)
        first = (block * groups_dev).astype(jnp.int32)
        indices = lax.dynamic_slice_in_dim(near_index, first, groups_dev, 0)
        counts = lax.dynamic_slice_in_dim(near_count, first, groups_dev, 0)
        weights = lax.dynamic_slice_in_dim(near_weight, first, groups_dev, 0)
        gathered = jnp.take(extended, indices.reshape(-1), axis=1).reshape(RHS, groups_dev, NEAR)
        live = jnp.arange(NEAR, dtype=jnp.int32)[None, :] < counts[:, None]
        gathered = jnp.where(live[None], gathered, jnp.zeros_like(gathered))
        correction = jnp.einsum('rgk,gtk->rgt', gathered.astype(jnp.float32), weights.astype(jnp.float32)).reshape(RHS, BLOCK)
        start = (block * BLOCK).astype(jnp.int32)
        current = lax.dynamic_slice_in_dim(field, start, BLOCK, 1)
        field = lax.dynamic_update_slice_in_dim(field, current + forward + correction, start, 1)
        return (field, None)
    field = jnp.zeros((RHS, PANELS), jnp.float32)
    field, _ = lax.scan(visit, field, jnp.arange(blocks, dtype=jnp.int32))
    scaled = (field * area[None, :]).T
    totals = jax.ops.segment_sum(scaled, conductor, num_segments=RHS).T
    return (field, totals)
```

```python
import functools

import jax
import jax.numpy as jnp
import numpy as np
from jax import lax
from jax.experimental import pallas as pl
from jax.experimental.pallas import tpu as pltpu
from jax.sharding import PartitionSpec as P

ROUNDS = 8
AXES = ("row", "col")
F32 = jnp.float32
BF16 = jnp.bfloat16

X, NORM, AREA, MEMBER, ONE = 0, 6, 9, 11, 12
FEATURES = 16
DEPTH = 32
VMEM_LIMIT = 48 * 2**20


def chooser(left):
    table = np.zeros((DEPTH, FEATURES), np.float32)
    row = 0
    for axis in range(3):
        for first in range(2):
            for second in range(2):
                feature = X + 2 * axis + (first if left else second)
                table[row, feature] = 1.0 if left else -2.0
                row += 1
    for term in range(3):
        table[row, NORM + term if left else ONE] = 1.0
        table[row + 3, ONE if left else NORM + term] = 1.0
        row += 1
    return jnp.asarray(table, BF16)


def in_vmem(body, out_shape, scratch=(), flops=0):
    return pl.pallas_call(
        body,
        out_shape=out_shape,
        scratch_shapes=list(scratch),
        compiler_params=pltpu.CompilerParams(vmem_limit_bytes=VMEM_LIMIT),
        cost_estimate=pl.CostEstimate(flops=flops, bytes_accessed=2**20, transcendentals=0),
    )


def rounded(value):
    return value.astype(BF16).astype(F32)


def bundle_body(geo_ref, charges_ref, conductor_ref, out_ref, rows_ref):
    rhs = charges_ref.shape[0]
    size = geo_ref[3:4, :]
    area = size * size
    out_ref[0:rhs, :] = (charges_ref[...].astype(F32) * area).astype(BF16)
    rows_ref[...] = jnp.zeros_like(rows_ref)
    norm = area
    for axis in range(3):
        value = geo_ref[axis : axis + 1, :]
        high = rounded(value)
        low = rounded(value - high)
        rows_ref[X + 2 * axis : X + 2 * axis + 1, :] = high
        rows_ref[X + 2 * axis + 1 : X + 2 * axis + 2, :] = low
        kept = high + low
        norm = norm + kept * kept
    for term in range(3):
        part = rounded(norm)
        rows_ref[NORM + term : NORM + term + 1, :] = part
        norm = norm - part
    high = rounded(area)
    rows_ref[AREA : AREA + 1, :] = high
    rows_ref[AREA + 1 : AREA + 2, :] = area - high
    rows_ref[MEMBER : MEMBER + 1, :] = conductor_ref[...].astype(F32)
    rows_ref[ONE : ONE + 1, :] = jnp.ones_like(area)
    out_ref[rhs:, :] = rows_ref[...].astype(BF16)


def make_bundle(geometry, charges, conductor):
    rhs, panels = charges.shape
    return in_vmem(
        bundle_body,
        jax.ShapeDtypeStruct((rhs + FEATURES, panels), BF16),
        [pltpu.VMEM((FEATURES, panels), F32)],
    )(geometry, charges, conductor.reshape(1, panels))


def left_side(features, table):
    return lax.dot_general(
        features, table, (((0,), (1,)), ((), ())), preferred_element_type=F32
    ).astype(BF16)


def right_side(features, table):
    return jnp.dot(table, features, preferred_element_type=F32).astype(BF16)


def tile_of(left, right):
    return lax.rsqrt(jnp.dot(left, right, preferred_element_type=F32)).astype(BF16)


def two_stage(steps, make, use, slots):
    slots[0][...] = make(0)

    @pl.loop(0, steps // 2 - 1)
    def _(half):
        step = 2 * half
        slots[1][...] = make(step + 1)
        use(step, slots[0][...])
        slots[0][...] = make(step + 2)
        use(step + 1, slots[1][...])

    slots[1][...] = make(steps - 1)
    use(steps - 2, slots[0][...])
    use(steps - 1, slots[1][...])


def totals_of(field, bundle):
    rhs = field.shape[0]
    features = bundle[rhs:, :].astype(F32)
    area = features[AREA : AREA + 1, :] + features[AREA + 1 : AREA + 2, :]
    names = lax.broadcasted_iota(jnp.int32, field.shape, 0).astype(F32)
    member = jnp.where(names == features[MEMBER : MEMBER + 1, :], 1.0, 0.0).astype(BF16)
    scaled = field * area
    high = scaled.astype(BF16)
    low = (scaled - high.astype(F32)).astype(BF16)
    dims = (((1,), (1,)), ((), ()))
    return lax.dot_general(high, member, dims, preferred_element_type=F32) + lax.dot_general(
        low, member, dims, preferred_element_type=F32
    )


def self_body(rowblk, own_ref, ltab_ref, rtab_ref, out_ref, left_ref, right_ref, *slots):
    rhs, panels = out_ref.shape
    features = own_ref[rhs:, :]
    left_ref[...] = left_side(features, ltab_ref[...])
    right_ref[...] = right_side(features, rtab_ref[...])
    out_ref[...] = jnp.zeros_like(out_ref)

    def make(step):
        start = pl.multiple_of(step * rowblk, rowblk)
        return tile_of(left_ref[pl.ds(start, rowblk), :], right_ref[...])

    def use(step, tile):
        start = pl.multiple_of(step * rowblk, rowblk)
        out_ref[...] += jnp.dot(
            own_ref[0:rhs, pl.ds(start, rowblk)], tile, preferred_element_type=F32
        )

    two_stage(panels // rowblk, make, use, slots)


def self_field(own, tables):
    rows, panels = own.shape
    rhs = rows - FEATURES
    rowblk = 256
    return in_vmem(
        functools.partial(self_body, rowblk),
        jax.ShapeDtypeStruct((rhs, panels), F32),
        [
            pltpu.VMEM((panels, DEPTH), BF16),
            pltpu.VMEM((DEPTH, panels), BF16),
            pltpu.VMEM((rowblk, panels), BF16),
            pltpu.VMEM((rowblk, panels), BF16),
        ],
        flops=2 * 400 * panels * panels,
    )(own, *tables)


def pairs_body(
    rowblk, last, pair_ref, far_ref, ltab_ref, rtab_ref, field_in, totals_in,
    field_ref, back_ref, totals_ref, left_ref, right_ref, sum_ref, *slots
):
    blocks, rhs, panels = field_ref.shape
    for block in range(blocks):
        left_ref[block] = left_side(far_ref[block, rhs:, :], ltab_ref[...])
        right_ref[block] = right_side(pair_ref[block, rhs:, :], rtab_ref[...])
    field_ref[...] = field_in[...]
    sum_ref[...] = jnp.zeros_like(sum_ref)
    chunks = panels // rowblk

    def place(step):
        turn = step // chunks
        start = pl.multiple_of((step % chunks) * rowblk, rowblk)
        return turn // blocks, turn % blocks, start

    def make(step):
        far, own, start = place(step)
        return tile_of(left_ref[far, pl.ds(start, rowblk), :], right_ref[own])

    def use(step, tile):
        far, own, start = place(step)
        field_ref[own] += jnp.dot(
            far_ref[far, 0:rhs, pl.ds(start, rowblk)], tile, preferred_element_type=F32
        )
        sum_ref[far, :, pl.ds(start, rowblk)] += lax.dot_general(
            pair_ref[own, 0:rhs, :], tile, (((1,), (1,)), ((), ())), preferred_element_type=F32
        )

    two_stage(blocks * blocks * chunks, make, use, slots)
    totals = totals_in[...]
    for block in range(blocks):
        totals = totals + totals_of(sum_ref[block], far_ref[block])
        if last:
            totals = totals + totals_of(field_ref[block], pair_ref[block])
    totals_ref[...] = totals
    back_ref[...] = sum_ref[...].astype(BF16)


def pairs_field(pair, far, tables, field, totals, last):
    blocks, rows, panels = pair.shape
    rhs = rows - FEATURES
    rowblk = 256
    return in_vmem(
        functools.partial(pairs_body, rowblk, last),
        (
            jax.ShapeDtypeStruct((blocks, rhs, panels), F32),
            jax.ShapeDtypeStruct((blocks, rhs, panels), BF16),
            jax.ShapeDtypeStruct(totals.shape, F32),
        ),
        [
            pltpu.VMEM((blocks, panels, DEPTH), BF16),
            pltpu.VMEM((blocks, DEPTH, panels), BF16),
            pltpu.VMEM((blocks, rhs, panels), F32),
            pltpu.VMEM((rowblk, panels), BF16),
            pltpu.VMEM((rowblk, panels), BF16),
        ],
        flops=2 * 400 * panels * panels * blocks * blocks,
    )(pair, far, *tables, field, totals)


def near_body(
    twin_ref, own_ref, other_ref, index_ref, count_ref, odd_ref, weight_ref, out_ref, ext_ref
):
    rhs, panels = own_ref.shape
    groups, near = index_ref.shape
    for side, ref in enumerate((twin_ref, own_ref, other_ref)):
        ext_ref[:, side * panels : (side + 1) * panels] = ref[...].astype(F32)
    turn = jnp.where(odd_ref[0] == 1, 0, 2 * panels)

    @pl.loop(0, groups)
    def _(group):
        index = index_ref[pl.ds(group, 1), :]
        moved = jnp.where(index < panels, index + turn, index)
        index = jnp.where(index >= 2 * panels, index - turn, moved)
        slot = lax.broadcasted_iota(jnp.int32, (1, near), 1)
        live = slot < count_ref[group]
        lane = jnp.broadcast_to(index % near, (rhs, near))
        piece = jnp.broadcast_to(jnp.where(live, index // near, -1), (rhs, near))
        taken = jnp.zeros((rhs, near), F32)
        for part in range(3 * panels // near):
            found = jnp.take_along_axis(
                ext_ref[:, part * near : (part + 1) * near], lane, axis=1
            )
            taken = jnp.where(piece == part, found, taken)
        width = weight_ref.shape[1]
        out_ref[:, pl.ds(pl.multiple_of(group * width, width), width)] = lax.dot_general(
            taken.astype(BF16), weight_ref[group], (((1,), (1,)), ((), ())),
            preferred_element_type=F32,
        )


def near_field(twin, own, other, index, count, odd, weight):
    rhs, panels = own.shape
    vmem = pl.BlockSpec(memory_space=pltpu.VMEM)
    return pl.pallas_call(
        near_body,
        out_shape=jax.ShapeDtypeStruct((rhs, panels), F32),
        in_specs=[vmem] * 4 + [pl.BlockSpec(memory_space=pltpu.SMEM)] * 2 + [vmem],
        out_specs=vmem,
        scratch_shapes=[pltpu.VMEM((rhs, 3 * panels), F32)],
        compiler_params=pltpu.CompilerParams(vmem_limit_bytes=VMEM_LIMIT),
        cost_estimate=pl.CostEstimate(flops=2 * 10**9, bytes_accessed=2**20, transcendentals=0),
    )(twin, own, other, index, count, odd, weight)


def start_body(self_ref, near_ref, field_ref):
    field_ref[0] = self_ref[...] + near_ref[...]
    field_ref[1] = jnp.zeros_like(self_ref)


def send(value, source_of):
    count = lax.axis_size(AXES)
    return lax.ppermute(value, AXES, [(source_of(d), d) for d in range(count)])


def send_back(value, source_of):
    count = lax.axis_size(AXES)
    return lax.ppermute(value, AXES, [(d, source_of(d)) for d in range(count)])


def paired_blocks(geometry, charges, near_index, near_count, near_weight, conductor):
    cols = lax.axis_size("col")
    core, flip_x, far_z = cols, 2 * cols, cols // 2
    rhs, panels = charges.shape

    def partner(d, far):
        second = bool(d & core)
        mask = 1 + (flip_x if bool(d & 1) != second else 0) + (2 if second else 0)
        return d ^ (mask + (far_z if far else 0))

    def other_neighbour(d):
        count = lax.axis_size(AXES)
        return (d + (1 if d & 1 else -1)) % count

    tables = (chooser(True), chooser(False))
    bundle = make_bundle(geometry, charges, conductor)
    sibling = send(bundle, lambda d: d ^ core)
    pair = jnp.stack([bundle, sibling])
    close = send(pair, lambda d: partner(d, False))
    far = send(pair, lambda d: partner(d, True))
    twin = send(charges, lambda d: d ^ 1)
    other = send(charges, other_neighbour)
    own = self_field(bundle, tables)
    odd = (lax.axis_index(AXES) % 2).reshape(1)
    near = near_field(twin, charges, other, near_index, near_count, odd, near_weight)
    pair_shape = (2, rhs, panels)
    field = in_vmem(start_body, jax.ShapeDtypeStruct(pair_shape, F32))(own, near)
    totals = jnp.zeros((rhs, rhs), F32)
    field, close_back, totals = pairs_field(pair, close, tables, field, totals, False)
    close_back = send_back(close_back, lambda d: partner(d, False))
    field, far_back, totals = pairs_field(pair, far, tables, field, totals, True)
    far_back = send_back(far_back, lambda d: partner(d, True))
    for step in (core, 1, flip_x, 2, far_z):
        totals = totals + send(totals, lambda d: d ^ step)
    back = close_back.astype(F32) + far_back.astype(F32)
    field = field + back
    twin_part = send(field[1].astype(BF16), lambda d: d ^ core)
    return (field[0] + twin_part.astype(F32), totals)


def passed_along(value, axis, steps):
    count = lax.axis_size(axis)
    pairs = [(source, (source + steps) % count) for source in range(count)]
    return lax.ppermute(value, axis, pairs)


def extended_2(x, sides, width):
    for axis, dim in sides:
        count, length = (lax.axis_size(axis), x.shape[dim])
        up = [(i, (i + 1) % count) for i in range(count)]
        down = [(j, i) for i, j in up]
        last = lax.slice_in_dim(x, length - width, length, axis=dim)
        initial = lax.slice_in_dim(x, 0, width, axis=dim)
        before = lax.ppermute(last, axis, up)
        after = lax.ppermute(initial, axis, down)
        x = jnp.concatenate([before, x, after], axis=dim)
    return x


def kernel_tile(rows, cols):
    delta_x = rows[0][:, None] - cols[0][None, :]
    delta_y = rows[1][:, None] - cols[1][None, :]
    delta_z = rows[2][:, None] - cols[2][None, :]
    spread = rows[3][:, None] * rows[3][:, None] + cols[3][None, :] * cols[3][None, :]
    squared = delta_x * delta_x + delta_y * delta_y + delta_z * delta_z + spread
    return lax.rsqrt(squared).astype(BF16)


def pair_products(own_geo, own_w, other_geo, other_w, backwards):
    panels = own_geo.shape[1]
    rowblk = min(256, panels)
    pieces = []
    back = jnp.zeros(other_w.shape, F32)
    for start in range(0, panels, rowblk):
        tile = kernel_tile(own_geo[:, start : start + rowblk], other_geo)
        pieces.append(
            lax.dot_general(
                other_w, tile, (((1,), (1,)), ((), ())), preferred_element_type=F32
            )
        )
        if backwards:
            back = back + jnp.dot(
                own_w[:, start : start + rowblk], tile, preferred_element_type=F32
            )
    return (jnp.concatenate(pieces, axis=1), back)


def from_lower(geometry, weighted, offset):
    geo = passed_along(geometry, ("row", "col"), offset)
    wts = passed_along(weighted, ("row", "col"), offset)
    return (geo, wts)


def give_back(partial_value, offset):
    return passed_along(partial_value, ("row", "col"), -offset)


def offset_rounds(geometry, charges, near_index, near_count, near_weight, conductor):
    devices = lax.axis_size(("row", "col"))
    stride = devices // (2 * ROUNDS)
    offsets = [1 + k * stride for k in range(ROUNDS)]
    panels = charges.shape[1]
    groups_dev = near_index.shape[0]
    area = geometry[3] * geometry[3]
    weighted = (charges.astype(F32) * area[None, :]).astype(BF16)
    field, unused = pair_products(geometry, weighted, geometry, weighted, False)
    for turn in range(ROUNDS):
        offset = offsets[turn]
        lower_geo, lower_w = from_lower(geometry, weighted, offset)
        forward, back = pair_products(geometry, weighted, lower_geo, lower_w, True)
        field = field + forward + give_back(back.astype(BF16), offset).astype(F32)
    extended = extended_2(charges, ((("row", "col"), 1),), panels)
    gathered = jnp.take(extended, near_index.reshape(-1), axis=1).reshape(
        charges.shape[0], groups_dev, near_index.shape[1]
    )
    live = jnp.arange(near_index.shape[1], dtype=jnp.int32)[None, :] < near_count[:, None]
    gathered = jnp.where(live[None], gathered, jnp.zeros_like(gathered))
    correction = jnp.einsum(
        "rgk,gtk->rgt", gathered, near_weight, preferred_element_type=F32
    )
    field = field + correction.reshape(charges.shape[0], panels)
    member = (conductor[:, None] == jnp.arange(charges.shape[0], dtype=jnp.int32)[None, :]).astype(
        F32
    )
    local_totals = jnp.dot(
        field * area[None, :],
        member,
        precision=lax.Precision.HIGHEST,
        preferred_element_type=F32,
    )
    totals = lax.psum(local_totals, ("row", "col"))
    return (field, totals)


def on_device(geometry, *rest):
    if lax.axis_size(AXES) == 4 * ROUNDS:
        return paired_blocks(geometry, *rest)
    return offset_rounds(geometry, *rest)


def solution(mesh):
    in_specs = (
        P(None, ("row", "col")),
        P(None, ("row", "col")),
        P(("row", "col"), None),
        P(("row", "col")),
        P(("row", "col"), None, None),
        P(("row", "col")),
    )
    out_specs = (P(None, ("row", "col")), P())
    return jax.shard_map(
        on_device, mesh=mesh, in_specs=in_specs, out_specs=out_specs, check_vma=False
    )
```

```python
import functools

import jax
import jax.numpy as jnp
import numpy as np
from jax import lax
from jax.experimental import pallas as pl
from jax.experimental.pallas import tpu as pltpu
from jax.sharding import PartitionSpec as P

ROUNDS = 8
AXES = ("row", "col")
F32 = jnp.float32
BF16 = jnp.bfloat16

X, NORM, AREA, MEMBER, ONE = 0, 6, 9, 11, 12
FEATURES = 16
DEPTH = 32
VMEM_LIMIT = 48 * 2**20


def chooser(left):
    table = np.zeros((DEPTH, FEATURES), np.float32)
    row = 0
    for axis in range(3):
        for first in range(2):
            for second in range(2):
                feature = X + 2 * axis + (first if left else second)
                table[row, feature] = 1.0 if left else -2.0
                row += 1
    for term in range(3):
        table[row, NORM + term if left else ONE] = 1.0
        table[row + 3, ONE if left else NORM + term] = 1.0
        row += 1
    return jnp.asarray(table, BF16)


def blocking(panels):
    rows = next((r for r in (384, 256, 128) if panels % (2 * r) == 0), panels // 2)
    return rows, 256 if panels % 256 == 0 else panels


def in_vmem(body, out_shape, scratch=(), flops=0):
    return pl.pallas_call(
        body,
        out_shape=out_shape,
        scratch_shapes=list(scratch),
        compiler_params=pltpu.CompilerParams(vmem_limit_bytes=VMEM_LIMIT),
        cost_estimate=pl.CostEstimate(flops=flops, bytes_accessed=2**10, transcendentals=0),
    )


def rounded(value):
    return value.astype(BF16).astype(F32)


def bundle_body(geo_ref, charges_ref, conductor_ref, out_ref, rows_ref):
    rhs = charges_ref.shape[0]
    size = geo_ref[3:4, :]
    area = size * size
    out_ref[0:rhs, :] = (charges_ref[...].astype(F32) * area).astype(BF16)
    rows_ref[...] = jnp.zeros_like(rows_ref)
    norm = area
    for axis in range(3):
        value = geo_ref[axis : axis + 1, :]
        high = rounded(value)
        low = rounded(value - high)
        rows_ref[X + 2 * axis : X + 2 * axis + 1, :] = high
        rows_ref[X + 2 * axis + 1 : X + 2 * axis + 2, :] = low
        kept = high + low
        norm = norm + kept * kept
    for term in range(3):
        part = rounded(norm)
        rows_ref[NORM + term : NORM + term + 1, :] = part
        norm = norm - part
    high = rounded(area)
    rows_ref[AREA : AREA + 1, :] = high
    rows_ref[AREA + 1 : AREA + 2, :] = area - high
    rows_ref[MEMBER : MEMBER + 1, :] = conductor_ref[...].astype(F32)
    rows_ref[ONE : ONE + 1, :] = jnp.ones_like(area)
    out_ref[rhs:, :] = rows_ref[...].astype(BF16)


def make_bundle(geometry, charges, conductor):
    rhs, panels = charges.shape
    return in_vmem(
        bundle_body,
        jax.ShapeDtypeStruct((rhs + FEATURES, panels), BF16),
        [pltpu.VMEM((FEATURES, panels), F32)],
    )(geometry, charges, conductor.reshape(1, panels))


def left_side(features, table):
    return lax.dot_general(
        features, table, (((0,), (1,)), ((), ())), preferred_element_type=F32
    ).astype(BF16)


def right_side(features, table):
    return jnp.dot(table, features, preferred_element_type=F32).astype(BF16)


def tile_of(left, right):
    return lax.rsqrt(jnp.dot(left, right, preferred_element_type=F32)).astype(BF16)


def two_stage(steps, make, use, slots, width):
    strips = range(0, slots[0].shape[1], width)

    def one(step, now, later):
        carry = None
        for start in strips:
            if later is not None:
                later[:, start : start + width] = make(step + 1, start)
            carry = use(step, now[:, start : start + width], start, carry)
        use(step, None, None, carry)

    for start in strips:
        slots[0][:, start : start + width] = make(0, start)

    @pl.loop(0, steps // 2 - 1)
    def _(half):
        one(2 * half, slots[0], slots[1])
        one(2 * half + 1, slots[1], slots[0])

    one(steps - 2, slots[0], slots[1])
    one(steps - 1, slots[1], None)


def totals_of(field, bundle):
    rhs = field.shape[0]
    features = bundle[rhs:, :].astype(F32)
    area = features[AREA : AREA + 1, :] + features[AREA + 1 : AREA + 2, :]
    names = lax.broadcasted_iota(jnp.int32, field.shape, 0).astype(F32)
    member = jnp.where(names == features[MEMBER : MEMBER + 1, :], 1.0, 0.0).astype(BF16)
    scaled = field * area
    high = scaled.astype(BF16)
    low = (scaled - high.astype(F32)).astype(BF16)
    dims = (((1,), (1,)), ((), ()))
    return lax.dot_general(high, member, dims, preferred_element_type=F32) + lax.dot_general(
        low, member, dims, preferred_element_type=F32
    )


def self_body(rowblk, width, own_ref, ltab_ref, rtab_ref, out_ref, left_ref, right_ref, *slots):
    _, rhs, panels = out_ref.shape
    features = own_ref[rhs:, :]
    left_ref[...] = left_side(features, ltab_ref[...])
    right_ref[...] = right_side(features, rtab_ref[...])
    out_ref[...] = jnp.zeros_like(out_ref)

    def make(step, strip):
        start = pl.multiple_of(step * rowblk, rowblk)
        return tile_of(left_ref[pl.ds(start, rowblk), :], right_ref[:, strip : strip + width])

    def use(step, tile, strip, carry):
        if tile is None:
            return
        start = pl.multiple_of(step * rowblk, rowblk)
        out_ref[0, :, strip : strip + width] += jnp.dot(
            own_ref[0:rhs, pl.ds(start, rowblk)], tile, preferred_element_type=F32
        )

    two_stage(panels // rowblk, make, use, slots, width)


def self_field(own, tables):
    rows, panels = own.shape
    rhs = rows - FEATURES
    rowblk, width = blocking(panels)
    return in_vmem(
        functools.partial(self_body, rowblk, width),
        jax.ShapeDtypeStruct((2, rhs, panels), F32),
        [
            pltpu.VMEM((panels, DEPTH), BF16),
            pltpu.VMEM((DEPTH, panels), BF16),
            pltpu.VMEM((rowblk, panels), BF16),
            pltpu.VMEM((rowblk, panels), BF16),
        ],
        flops=0,
    )(own, *tables)


def pairs_body(
    rowblk, width, last, pair_ref, far_ref, ltab_ref, rtab_ref, field_in, totals_in,
    field_ref, back_ref, totals_ref, left_ref, right_ref, sum_ref, *slots
):
    blocks, rhs, panels = field_ref.shape
    for block in range(blocks):
        left_ref[block] = left_side(far_ref[block, rhs:, :], ltab_ref[...])
        right_ref[block] = right_side(pair_ref[block, rhs:, :], rtab_ref[...])
    field_ref[...] = field_in[...]
    sum_ref[...] = jnp.zeros_like(sum_ref)
    chunks = panels // rowblk

    def place(step):
        turn = step // chunks
        start = pl.multiple_of((step % chunks) * rowblk, rowblk)
        return turn // blocks, turn % blocks, start

    def make(step, strip):
        far, own, start = place(step)
        return tile_of(
            left_ref[far, pl.ds(start, rowblk), :], right_ref[own, :, strip : strip + width]
        )

    def use(step, tile, strip, carry):
        far, own, start = place(step)
        if tile is None:
            sum_ref[far, :, pl.ds(start, rowblk)] += carry
            return
        part = lax.dot_general(
            pair_ref[own, 0:rhs, strip : strip + width], tile, (((1,), (1,)), ((), ())),
            preferred_element_type=F32,
        )
        field_ref[own, :, strip : strip + width] += jnp.dot(
            far_ref[far, 0:rhs, pl.ds(start, rowblk)], tile, preferred_element_type=F32
        )
        return part if carry is None else carry + part

    two_stage(blocks * blocks * chunks, make, use, slots, width)
    totals = totals_in[...]
    for block in range(blocks):
        totals = totals + totals_of(sum_ref[block], far_ref[block])
        if last:
            totals = totals + totals_of(field_ref[block], pair_ref[block])
    totals_ref[...] = totals
    back_ref[...] = sum_ref[...].astype(BF16)


def pairs_field(pair, far, tables, field, totals, last):
    blocks, rows, panels = pair.shape
    rhs = rows - FEATURES
    rowblk, width = blocking(panels)
    work = 800 * panels * panels * blocks * blocks
    return in_vmem(
        functools.partial(pairs_body, rowblk, width, last),
        (
            jax.ShapeDtypeStruct((blocks, rhs, panels), F32),
            jax.ShapeDtypeStruct((blocks, rhs, panels), BF16),
            jax.ShapeDtypeStruct(totals.shape, F32),
        ),
        [
            pltpu.VMEM((blocks, panels, DEPTH), BF16),
            pltpu.VMEM((blocks, DEPTH, panels), BF16),
            pltpu.VMEM((blocks, rhs, panels), F32),
            pltpu.VMEM((rowblk, panels), BF16),
            pltpu.VMEM((rowblk, panels), BF16),
        ],
        flops=work if last else 0,
    )(pair, far, *tables, field, totals)


def near_body(
    twin_ref, own_ref, other_ref, index_ref, count_ref, odd_ref, weight_ref, field_in,
    field_ref, ext_ref
):
    rhs, panels = own_ref.shape
    groups, near = index_ref.shape
    for side, ref in enumerate((twin_ref, own_ref, other_ref)):
        ext_ref[:, side * panels : (side + 1) * panels] = ref[...].astype(F32)
    field_ref[...] = field_in[...]
    turn = jnp.where(odd_ref[0] == 1, 0, 2 * panels)

    @pl.loop(0, groups)
    def _(group):
        index = index_ref[pl.ds(group, 1), :]
        moved = jnp.where(index < panels, index + turn, index)
        index = jnp.where(index >= 2 * panels, index - turn, moved)
        slot = lax.broadcasted_iota(jnp.int32, (1, near), 1)
        live = slot < count_ref[group]
        lane = jnp.broadcast_to(index % near, (rhs, near))
        piece = jnp.broadcast_to(jnp.where(live, index // near, -1), (rhs, near))
        taken = jnp.zeros((rhs, near), F32)
        for part in range(3 * panels // near):
            found = jnp.take_along_axis(
                ext_ref[:, part * near : (part + 1) * near], lane, axis=1
            )
            taken = jnp.where(piece == part, found, taken)
        width = weight_ref.shape[1]
        field_ref[0, :, pl.ds(pl.multiple_of(group * width, width), width)] += lax.dot_general(
            taken.astype(BF16), weight_ref[group], (((1,), (1,)), ((), ())),
            preferred_element_type=F32,
        )


def near_field(twin, own, other, index, count, odd, weight, field):
    rhs, panels = own.shape
    vmem = pl.BlockSpec(memory_space=pltpu.VMEM)
    return pl.pallas_call(
        near_body,
        out_shape=jax.ShapeDtypeStruct(field.shape, F32),
        in_specs=[vmem] * 4 + [pl.BlockSpec(memory_space=pltpu.SMEM)] * 2 + [vmem] * 2,
        out_specs=vmem,
        scratch_shapes=[pltpu.VMEM((rhs, 3 * panels), F32)],
        compiler_params=pltpu.CompilerParams(vmem_limit_bytes=VMEM_LIMIT),
        cost_estimate=pl.CostEstimate(flops=0, bytes_accessed=2**10, transcendentals=0),
    )(twin, own, other, index, count, odd, weight, field)


def send(value, source_of):
    count = lax.axis_size(AXES)
    return lax.ppermute(value, AXES, [(source_of(d), d) for d in range(count)])


def send_back(value, source_of):
    count = lax.axis_size(AXES)
    return lax.ppermute(value, AXES, [(d, source_of(d)) for d in range(count)])


def paired_blocks(geometry, charges, near_index, near_count, near_weight, conductor):
    cols = lax.axis_size("col")
    core, flip_x, far_z = cols, 2 * cols, cols // 2
    rhs = charges.shape[0]

    def partner(d, far):
        second = bool(d & core)
        mask = 1 + (flip_x if bool(d & 1) != second else 0) + (2 if second else 0)
        return d ^ (mask + (far_z if far else 0))

    def other_neighbour(d):
        count = lax.axis_size(AXES)
        return (d + (1 if d & 1 else -1)) % count

    tables = (chooser(True), chooser(False))
    bundle = make_bundle(geometry, charges, conductor)
    sibling = send(bundle, lambda d: d ^ core)
    pair = jnp.stack([bundle, sibling])
    close = send(pair, lambda d: partner(d, False))
    far = send(pair, lambda d: partner(d, True))
    twin = send(charges, lambda d: d ^ 1)
    other = send(charges, other_neighbour)
    odd = (lax.axis_index(AXES) % 2).reshape(1)
    field = self_field(bundle, tables)
    totals = jnp.zeros((rhs, rhs), F32)
    field, close_back, totals = pairs_field(pair, close, tables, field, totals, False)
    field = near_field(twin, charges, other, near_index, near_count, odd, near_weight, field)
    close_back = send_back(close_back, lambda d: partner(d, False))
    field, far_back, totals = pairs_field(pair, far, tables, field, totals, True)
    far_back = send_back(far_back, lambda d: partner(d, True))
    close_back, totals = lax.optimization_barrier((close_back, totals))
    for step in (core, 1, flip_x):
        totals = totals + send(totals, lambda d: d ^ step)
    far_back, totals = lax.optimization_barrier((far_back, totals))
    back = close_back.astype(F32) + far_back.astype(F32)
    field = field + back
    twin_part = send(field[1].astype(BF16), lambda d: d ^ core)
    for step in (2, far_z):
        totals = totals + send(totals, lambda d: d ^ step)
    return (field[0] + twin_part.astype(F32), totals)


def passed_along(value, axis, steps):
    count = lax.axis_size(axis)
    pairs = [(source, (source + steps) % count) for source in range(count)]
    return lax.ppermute(value, axis, pairs)


def extended_2(x, sides, width):
    for axis, dim in sides:
        count, length = (lax.axis_size(axis), x.shape[dim])
        up = [(i, (i + 1) % count) for i in range(count)]
        down = [(j, i) for i, j in up]
        last = lax.slice_in_dim(x, length - width, length, axis=dim)
        initial = lax.slice_in_dim(x, 0, width, axis=dim)
        before = lax.ppermute(last, axis, up)
        after = lax.ppermute(initial, axis, down)
        x = jnp.concatenate([before, x, after], axis=dim)
    return x


def kernel_tile(rows, cols):
    delta_x = rows[0][:, None] - cols[0][None, :]
    delta_y = rows[1][:, None] - cols[1][None, :]
    delta_z = rows[2][:, None] - cols[2][None, :]
    spread = rows[3][:, None] * rows[3][:, None] + cols[3][None, :] * cols[3][None, :]
    squared = delta_x * delta_x + delta_y * delta_y + delta_z * delta_z + spread
    return lax.rsqrt(squared).astype(BF16)


def pair_products(own_geo, own_w, other_geo, other_w, backwards):
    panels = own_geo.shape[1]
    rowblk = min(256, panels)
    pieces = []
    back = jnp.zeros(other_w.shape, F32)
    for start in range(0, panels, rowblk):
        tile = kernel_tile(own_geo[:, start : start + rowblk], other_geo)
        pieces.append(
            lax.dot_general(
                other_w, tile, (((1,), (1,)), ((), ())), preferred_element_type=F32
            )
        )
        if backwards:
            back = back + jnp.dot(
                own_w[:, start : start + rowblk], tile, preferred_element_type=F32
            )
    return (jnp.concatenate(pieces, axis=1), back)


def from_lower(geometry, weighted, offset):
    geo = passed_along(geometry, ("row", "col"), offset)
    wts = passed_along(weighted, ("row", "col"), offset)
    return (geo, wts)


def give_back(partial_value, offset):
    return passed_along(partial_value, ("row", "col"), -offset)


def offset_rounds(geometry, charges, near_index, near_count, near_weight, conductor):
    devices = lax.axis_size(("row", "col"))
    stride = devices // (2 * ROUNDS)
    offsets = [1 + k * stride for k in range(ROUNDS)]
    panels = charges.shape[1]
    groups_dev = near_index.shape[0]
    area = geometry[3] * geometry[3]
    weighted = (charges.astype(F32) * area[None, :]).astype(BF16)
    field, unused = pair_products(geometry, weighted, geometry, weighted, False)
    for turn in range(ROUNDS):
        offset = offsets[turn]
        lower_geo, lower_w = from_lower(geometry, weighted, offset)
        forward, back = pair_products(geometry, weighted, lower_geo, lower_w, True)
        field = field + forward + give_back(back.astype(BF16), offset).astype(F32)
    extended = extended_2(charges, ((("row", "col"), 1),), panels)
    gathered = jnp.take(extended, near_index.reshape(-1), axis=1).reshape(
        charges.shape[0], groups_dev, near_index.shape[1]
    )
    live = jnp.arange(near_index.shape[1], dtype=jnp.int32)[None, :] < near_count[:, None]
    gathered = jnp.where(live[None], gathered, jnp.zeros_like(gathered))
    correction = jnp.einsum(
        "rgk,gtk->rgt", gathered, near_weight, preferred_element_type=F32
    )
    field = field + correction.reshape(charges.shape[0], panels)
    member = (conductor[:, None] == jnp.arange(charges.shape[0], dtype=jnp.int32)[None, :]).astype(
        F32
    )
    local_totals = jnp.dot(
        field * area[None, :],
        member,
        precision=lax.Precision.HIGHEST,
        preferred_element_type=F32,
    )
    totals = lax.psum(local_totals, ("row", "col"))
    return (field, totals)


def on_device(geometry, *rest):
    if lax.axis_size(AXES) == 4 * ROUNDS:
        return paired_blocks(geometry, *rest)
    return offset_rounds(geometry, *rest)


def solution(mesh):
    in_specs = (
        P(None, ("row", "col")),
        P(None, ("row", "col")),
        P(("row", "col"), None),
        P(("row", "col")),
        P(("row", "col"), None, None),
        P(("row", "col")),
    )
    out_specs = (P(None, ("row", "col")), P())
    return jax.shard_map(
        on_device, mesh=mesh, in_specs=in_specs, out_specs=out_specs, check_vma=False
    )
```

```python
import functools

import jax
import jax.numpy as jnp
import numpy as np
from jax import lax
from jax.experimental import pallas as pl
from jax.experimental.pallas import tpu as pltpu
from jax.sharding import PartitionSpec as P

ROUNDS = 8
AXES = ("row", "col")
F32 = jnp.float32
BF16 = jnp.bfloat16

X, NORM, AREA, MEMBER, ONE = 0, 6, 9, 11, 12
FEATURES = 16
DEPTH = 32
VMEM_LIMIT = 48 * 2**20


def chooser(left):
    table = np.zeros((DEPTH, FEATURES), np.float32)
    row = 0
    for axis in range(3):
        for first in range(2):
            for second in range(2):
                feature = X + 2 * axis + (first if left else second)
                table[row, feature] = 1.0 if left else -2.0
                row += 1
    for term in range(3):
        table[row, NORM + term if left else ONE] = 1.0
        table[row + 3, ONE if left else NORM + term] = 1.0
        row += 1
    return jnp.asarray(table, BF16)


def blocking(panels):
    rows = next((r for r in (384, 256, 128) if panels % (2 * r) == 0), panels // 2)
    return rows, 256 if panels % 256 == 0 else panels


def in_vmem(body, out_shape, scratch=(), flops=0):
    return pl.pallas_call(
        body,
        out_shape=out_shape,
        scratch_shapes=list(scratch),
        compiler_params=pltpu.CompilerParams(vmem_limit_bytes=VMEM_LIMIT),
        cost_estimate=pl.CostEstimate(flops=flops, bytes_accessed=2**10, transcendentals=0),
    )


def rounded(value):
    return value.astype(BF16).astype(F32)


def bundle_body(geo_ref, charges_ref, conductor_ref, out_ref, rows_ref):
    rhs = charges_ref.shape[0]
    size = geo_ref[3:4, :]
    area = size * size
    out_ref[0:rhs, :] = (charges_ref[...].astype(F32) * area).astype(BF16)
    rows_ref[...] = jnp.zeros_like(rows_ref)
    norm = area
    for axis in range(3):
        value = geo_ref[axis : axis + 1, :]
        high = rounded(value)
        low = rounded(value - high)
        rows_ref[X + 2 * axis : X + 2 * axis + 1, :] = high
        rows_ref[X + 2 * axis + 1 : X + 2 * axis + 2, :] = low
        kept = high + low
        norm = norm + kept * kept
    for term in range(3):
        part = rounded(norm)
        rows_ref[NORM + term : NORM + term + 1, :] = part
        norm = norm - part
    high = rounded(area)
    rows_ref[AREA : AREA + 1, :] = high
    rows_ref[AREA + 1 : AREA + 2, :] = area - high
    rows_ref[MEMBER : MEMBER + 1, :] = conductor_ref[...].astype(F32)
    rows_ref[ONE : ONE + 1, :] = jnp.ones_like(area)
    out_ref[rhs:, :] = rows_ref[...].astype(BF16)


def make_bundle(geometry, charges, conductor):
    rhs, panels = charges.shape
    return in_vmem(
        bundle_body,
        jax.ShapeDtypeStruct((rhs + FEATURES, panels), BF16),
        [pltpu.VMEM((FEATURES, panels), F32)],
    )(geometry, charges, conductor.reshape(1, panels))


def left_side(features, table):
    return lax.dot_general(
        features, table, (((0,), (1,)), ((), ())), preferred_element_type=F32
    ).astype(BF16)


def right_side(features, table):
    return jnp.dot(table, features, preferred_element_type=F32).astype(BF16)


def tile_of(left, right):
    return lax.rsqrt(jnp.dot(left, right, preferred_element_type=F32)).astype(BF16)


def two_stage(steps, make, use, slots, width):
    strips = range(0, slots[0].shape[1], width)

    def one(step, now, later):
        carry = None
        for start in strips:
            if later is not None:
                later[:, start : start + width] = make(step + 1, start)
            carry = use(step, now[:, start : start + width], start, carry)
        use(step, None, None, carry)

    for start in strips:
        slots[0][:, start : start + width] = make(0, start)

    @pl.loop(0, steps // 2 - 1)
    def _(half):
        one(2 * half, slots[0], slots[1])
        one(2 * half + 1, slots[1], slots[0])

    one(steps - 2, slots[0], slots[1])
    one(steps - 1, slots[1], None)


def totals_of(field, bundle):
    rhs = field.shape[0]
    features = bundle[rhs:, :].astype(F32)
    area = features[AREA : AREA + 1, :] + features[AREA + 1 : AREA + 2, :]
    names = lax.broadcasted_iota(jnp.int32, field.shape, 0).astype(F32)
    member = jnp.where(names == features[MEMBER : MEMBER + 1, :], 1.0, 0.0).astype(BF16)
    scaled = field * area
    high = scaled.astype(BF16)
    low = (scaled - high.astype(F32)).astype(BF16)
    dims = (((1,), (1,)), ((), ()))
    return lax.dot_general(high, member, dims, preferred_element_type=F32) + lax.dot_general(
        low, member, dims, preferred_element_type=F32
    )


def self_body(rowblk, width, own_ref, ltab_ref, rtab_ref, out_ref, left_ref, right_ref, *slots):
    _, rhs, panels = out_ref.shape
    features = own_ref[rhs:, :]
    left_ref[...] = left_side(features, ltab_ref[...])
    right_ref[...] = right_side(features, rtab_ref[...])
    out_ref[...] = jnp.zeros_like(out_ref)

    def make(step, strip):
        start = pl.multiple_of(step * rowblk, rowblk)
        return tile_of(left_ref[pl.ds(start, rowblk), :], right_ref[:, strip : strip + width])

    def use(step, tile, strip, carry):
        if tile is None:
            return
        start = pl.multiple_of(step * rowblk, rowblk)
        out_ref[0, :, strip : strip + width] += jnp.dot(
            own_ref[0:rhs, pl.ds(start, rowblk)], tile, preferred_element_type=F32
        )

    two_stage(panels // rowblk, make, use, slots, width)


def self_field(own, tables):
    rows, panels = own.shape
    rhs = rows - FEATURES
    rowblk, width = blocking(panels)
    return in_vmem(
        functools.partial(self_body, rowblk, width),
        jax.ShapeDtypeStruct((2, rhs, panels), F32),
        [
            pltpu.VMEM((panels, DEPTH), BF16),
            pltpu.VMEM((DEPTH, panels), BF16),
            pltpu.VMEM((rowblk, panels), BF16),
            pltpu.VMEM((rowblk, panels), BF16),
        ],
        flops=0,
    )(own, *tables)


def pairs_body(
    rowblk, width, pair_ref, far_ref, ltab_ref, rtab_ref, field_in, totals_in,
    field_ref, back_ref, totals_ref, left_ref, right_ref, sum_ref, *slots
):
    blocks, rhs, panels = field_ref.shape
    for block in range(blocks):
        left_ref[block] = left_side(far_ref[block, rhs:, :], ltab_ref[...])
        right_ref[block] = right_side(pair_ref[block, rhs:, :], rtab_ref[...])
    field_ref[...] = field_in[...]
    sum_ref[...] = jnp.zeros_like(sum_ref)
    chunks = panels // rowblk

    def place(step):
        turn = step // chunks
        start = pl.multiple_of((step % chunks) * rowblk, rowblk)
        return turn // blocks, turn % blocks, start

    def make(step, strip):
        far, own, start = place(step)
        return tile_of(
            left_ref[far, pl.ds(start, rowblk), :], right_ref[own, :, strip : strip + width]
        )

    def use(step, tile, strip, carry):
        far, own, start = place(step)
        if tile is None:
            sum_ref[far, :, pl.ds(start, rowblk)] += carry
            return
        part = lax.dot_general(
            pair_ref[own, 0:rhs, strip : strip + width], tile, (((1,), (1,)), ((), ())),
            preferred_element_type=F32,
        )
        field_ref[own, :, strip : strip + width] += jnp.dot(
            far_ref[far, 0:rhs, pl.ds(start, rowblk)], tile, preferred_element_type=F32
        )
        return part if carry is None else carry + part

    two_stage(blocks * blocks * chunks, make, use, slots, width)
    totals = totals_in[...]
    for block in range(blocks):
        totals = totals + totals_of(sum_ref[block], far_ref[block])
    totals_ref[...] = totals
    back_ref[...] = sum_ref[...].astype(BF16)


def pairs_field(pair, far, tables, field, totals, last):
    blocks, rows, panels = pair.shape
    rhs = rows - FEATURES
    rowblk, width = blocking(panels)
    work = 800 * panels * panels * blocks * blocks
    return in_vmem(
        functools.partial(pairs_body, rowblk, width),
        (
            jax.ShapeDtypeStruct((blocks, rhs, panels), F32),
            jax.ShapeDtypeStruct((blocks, rhs, panels), BF16),
            jax.ShapeDtypeStruct(totals.shape, F32),
        ),
        [
            pltpu.VMEM((blocks, panels, DEPTH), BF16),
            pltpu.VMEM((blocks, DEPTH, panels), BF16),
            pltpu.VMEM((blocks, rhs, panels), F32),
            pltpu.VMEM((rowblk, panels), BF16),
            pltpu.VMEM((rowblk, panels), BF16),
        ],
        flops=work if last else 0,
    )(pair, far, *tables, field, totals)


def near_body(
    twin_ref, own_ref, other_ref, index_ref, count_ref, odd_ref, weight_ref, field_in, totals_in,
    pair_ref, field_ref, totals_ref, ext_ref
):
    rhs, panels = own_ref.shape
    groups, near = index_ref.shape
    for side, ref in enumerate((twin_ref, own_ref, other_ref)):
        ext_ref[:, side * panels : (side + 1) * panels] = ref[...].astype(F32)
    field_ref[...] = field_in[...]
    turn = jnp.where(odd_ref[0] == 1, 0, 2 * panels)

    @pl.loop(0, groups)
    def _(group):
        index = index_ref[pl.ds(group, 1), :]
        moved = jnp.where(index < panels, index + turn, index)
        index = jnp.where(index >= 2 * panels, index - turn, moved)
        slot = lax.broadcasted_iota(jnp.int32, (1, near), 1)
        live = slot < count_ref[group]
        lane = jnp.broadcast_to(index % near, (rhs, near))
        piece = jnp.broadcast_to(jnp.where(live, index // near, -1), (rhs, near))
        taken = jnp.zeros((rhs, near), F32)
        for part in range(3 * panels // near):
            found = jnp.take_along_axis(
                ext_ref[:, part * near : (part + 1) * near], lane, axis=1
            )
            taken = jnp.where(piece == part, found, taken)
        width = weight_ref.shape[1]
        field_ref[0, :, pl.ds(pl.multiple_of(group * width, width), width)] += lax.dot_general(
            taken.astype(BF16), weight_ref[group], (((1,), (1,)), ((), ())),
            preferred_element_type=F32,
        )

    totals = totals_in[...]
    for block in range(field_ref.shape[0]):
        totals = totals + totals_of(field_ref[block], pair_ref[block])
    height = totals_ref.shape[1]
    flat = jnp.concatenate([totals[r : r + height, :] for r in range(0, rhs, height)], axis=1)
    totals_ref[...] = jnp.broadcast_to(flat[None], totals_ref.shape)


def near_field(twin, own, other, index, count, odd, weight, field, totals, pair):
    rhs, panels = own.shape
    vmem = pl.BlockSpec(memory_space=pltpu.VMEM)
    return pl.pallas_call(
        near_body,
        out_shape=(
            jax.ShapeDtypeStruct(field.shape, F32),
            jax.ShapeDtypeStruct((lax.axis_size(AXES), rhs * rhs // 128, 128), F32),
        ),
        in_specs=[vmem] * 4 + [pl.BlockSpec(memory_space=pltpu.SMEM)] * 2 + [vmem] * 4,
        out_specs=(vmem, vmem),
        scratch_shapes=[pltpu.VMEM((rhs, 3 * panels), F32)],
        compiler_params=pltpu.CompilerParams(vmem_limit_bytes=VMEM_LIMIT),
        cost_estimate=pl.CostEstimate(flops=4 * 10**9, bytes_accessed=2**10, transcendentals=0),
    )(twin, own, other, index, count, odd, weight, field, totals, pair)


def finish_body(field_ref, part_ref, totals_ref, potential_out, totals_out):
    potential_out[...] = field_ref[0] + part_ref[...].astype(F32)
    total = jnp.sum(totals_ref[...], axis=0)
    rhs, height = totals_out.shape[0], total.shape[0]
    for turn in range(rhs // height):
        totals_out[turn * height : (turn + 1) * height, :] = total[:, turn * rhs : (turn + 1) * rhs]


def send(value, source_of):
    count = lax.axis_size(AXES)
    return lax.ppermute(value, AXES, [(source_of(d), d) for d in range(count)])


def send_back(value, source_of):
    count = lax.axis_size(AXES)
    return lax.ppermute(value, AXES, [(d, source_of(d)) for d in range(count)])


def paired_blocks(geometry, charges, near_index, near_count, near_weight, conductor):
    cols = lax.axis_size("col")
    core, flip_x, far_z = cols, 2 * cols, cols // 2
    rhs = charges.shape[0]

    def partner(d, far):
        second = bool(d & core)
        mask = 1 + (flip_x if bool(d & 1) != second else 0) + (2 if second else 0)
        return d ^ (mask + (far_z if far else 0))

    def other_neighbour(d):
        count = lax.axis_size(AXES)
        return (d + (1 if d & 1 else -1)) % count

    tables = (chooser(True), chooser(False))
    bundle = make_bundle(geometry, charges, conductor)
    sibling = send(bundle, lambda d: d ^ core)
    pair = jnp.stack([bundle, sibling])
    close = send(pair, lambda d: partner(d, False))
    field = self_field(bundle, tables)
    late_pair, field = lax.optimization_barrier((pair, field))
    far = send(late_pair, lambda d: partner(d, True))
    odd = (lax.axis_index(AXES) % 2).reshape(1)
    totals = jnp.zeros((rhs, rhs), F32)
    field, close_back, totals = pairs_field(pair, close, tables, field, totals, False)
    close_back = send_back(close_back, lambda d: partner(d, False))
    late_charges, field = lax.optimization_barrier((charges, field))
    twin = send(late_charges, lambda d: d ^ 1)
    other = send(late_charges, other_neighbour)
    field, far_back, totals = pairs_field(pair, far, tables, field, totals, True)
    far_back = send_back(far_back, lambda d: partner(d, True))
    field, totals = near_field(
        twin, charges, other, near_index, near_count, odd, near_weight, field, totals, pair
    )
    close_back, totals = lax.optimization_barrier((close_back, totals))
    totals = lax.all_to_all(totals, AXES, 0, 0, tiled=True)
    field = field + close_back.astype(F32) + far_back.astype(F32)
    twin_part = send(field[1].astype(BF16), lambda d: d ^ core)
    return in_vmem(
        finish_body,
        (jax.ShapeDtypeStruct(charges.shape, F32), jax.ShapeDtypeStruct((rhs, rhs), F32)),
    )(field, twin_part, totals)


def passed_along(value, axis, steps):
    count = lax.axis_size(axis)
    pairs = [(source, (source + steps) % count) for source in range(count)]
    return lax.ppermute(value, axis, pairs)


def extended_2(x, sides, width):
    for axis, dim in sides:
        count, length = (lax.axis_size(axis), x.shape[dim])
        up = [(i, (i + 1) % count) for i in range(count)]
        down = [(j, i) for i, j in up]
        last = lax.slice_in_dim(x, length - width, length, axis=dim)
        initial = lax.slice_in_dim(x, 0, width, axis=dim)
        before = lax.ppermute(last, axis, up)
        after = lax.ppermute(initial, axis, down)
        x = jnp.concatenate([before, x, after], axis=dim)
    return x


def kernel_tile(rows, cols):
    delta_x = rows[0][:, None] - cols[0][None, :]
    delta_y = rows[1][:, None] - cols[1][None, :]
    delta_z = rows[2][:, None] - cols[2][None, :]
    spread = rows[3][:, None] * rows[3][:, None] + cols[3][None, :] * cols[3][None, :]
    squared = delta_x * delta_x + delta_y * delta_y + delta_z * delta_z + spread
    return lax.rsqrt(squared).astype(BF16)


def pair_products(own_geo, own_w, other_geo, other_w, backwards):
    panels = own_geo.shape[1]
    rowblk = min(256, panels)
    pieces = []
    back = jnp.zeros(other_w.shape, F32)
    for start in range(0, panels, rowblk):
        tile = kernel_tile(own_geo[:, start : start + rowblk], other_geo)
        pieces.append(
            lax.dot_general(
                other_w, tile, (((1,), (1,)), ((), ())), preferred_element_type=F32
            )
        )
        if backwards:
            back = back + jnp.dot(
                own_w[:, start : start + rowblk], tile, preferred_element_type=F32
            )
    return (jnp.concatenate(pieces, axis=1), back)


def from_lower(geometry, weighted, offset):
    geo = passed_along(geometry, ("row", "col"), offset)
    wts = passed_along(weighted, ("row", "col"), offset)
    return (geo, wts)


def give_back(partial_value, offset):
    return passed_along(partial_value, ("row", "col"), -offset)


def offset_rounds(geometry, charges, near_index, near_count, near_weight, conductor):
    devices = lax.axis_size(("row", "col"))
    stride = devices // (2 * ROUNDS)
    offsets = [1 + k * stride for k in range(ROUNDS)]
    panels = charges.shape[1]
    groups_dev = near_index.shape[0]
    area = geometry[3] * geometry[3]
    weighted = (charges.astype(F32) * area[None, :]).astype(BF16)
    field, unused = pair_products(geometry, weighted, geometry, weighted, False)
    for turn in range(ROUNDS):
        offset = offsets[turn]
        lower_geo, lower_w = from_lower(geometry, weighted, offset)
        forward, back = pair_products(geometry, weighted, lower_geo, lower_w, True)
        field = field + forward + give_back(back.astype(BF16), offset).astype(F32)
    extended = extended_2(charges, ((("row", "col"), 1),), panels)
    gathered = jnp.take(extended, near_index.reshape(-1), axis=1).reshape(
        charges.shape[0], groups_dev, near_index.shape[1]
    )
    live = jnp.arange(near_index.shape[1], dtype=jnp.int32)[None, :] < near_count[:, None]
    gathered = jnp.where(live[None], gathered, jnp.zeros_like(gathered))
    correction = jnp.einsum(
        "rgk,gtk->rgt", gathered, near_weight, preferred_element_type=F32
    )
    field = field + correction.reshape(charges.shape[0], panels)
    member = (conductor[:, None] == jnp.arange(charges.shape[0], dtype=jnp.int32)[None, :]).astype(
        F32
    )
    local_totals = jnp.dot(
        field * area[None, :],
        member,
        precision=lax.Precision.HIGHEST,
        preferred_element_type=F32,
    )
    totals = lax.psum(local_totals, ("row", "col"))
    return (field, totals)


def on_device(geometry, *rest):
    if lax.axis_size(AXES) == 4 * ROUNDS:
        return paired_blocks(geometry, *rest)
    return offset_rounds(geometry, *rest)


def solution(mesh):
    in_specs = (
        P(None, ("row", "col")),
        P(None, ("row", "col")),
        P(("row", "col"), None),
        P(("row", "col")),
        P(("row", "col"), None, None),
        P(("row", "col")),
    )
    out_specs = (P(None, ("row", "col")), P())
    return jax.shard_map(
        on_device, mesh=mesh, in_specs=in_specs, out_specs=out_specs, check_vma=False
    )
```

```python
import functools

import jax
import jax.numpy as jnp
import numpy as np
from jax import lax
from jax.experimental import pallas as pl
from jax.experimental.pallas import tpu as pltpu
from jax.sharding import PartitionSpec as P

ROUNDS = 8
AXES = ("row", "col")
F32 = jnp.float32
BF16 = jnp.bfloat16

X, NORM, AREA, MEMBER, ONE = 0, 6, 9, 11, 12
FEATURES = 16
LANES = 128
DEPTH = 32
VMEM_LIMIT = 48 * 2**20


def chooser(left):
    table = np.zeros((DEPTH, FEATURES), np.float32)
    row = 0
    for axis in range(3):
        for first in range(2):
            for second in range(2):
                feature = X + 2 * axis + (first if left else second)
                table[row, feature] = 1.0 if left else -2.0
                row += 1
    for term in range(3):
        table[row, NORM + term if left else ONE] = 1.0
        table[row + 3, ONE if left else NORM + term] = 1.0
        row += 1
    return jnp.asarray(table, BF16)


def blocking(panels):
    rows = next((r for r in (384, 256, 128) if panels % (2 * r) == 0), panels // 2)
    return rows, 256 if panels % 256 == 0 else panels


def in_vmem(body, out_shape, scratch=(), flops=0):
    return pl.pallas_call(
        body,
        out_shape=out_shape,
        scratch_shapes=list(scratch),
        compiler_params=pltpu.CompilerParams(vmem_limit_bytes=VMEM_LIMIT),
        cost_estimate=pl.CostEstimate(flops=flops, bytes_accessed=2**10, transcendentals=0),
    )


def rounded(value):
    return value.astype(BF16).astype(F32)


def bundle_body(geo_ref, charges_ref, conductor_ref, out_ref, rows_ref):
    rhs = charges_ref.shape[0]
    size = geo_ref[3:4, :]
    area = size * size
    out_ref[0:rhs, :] = (charges_ref[...].astype(F32) * area).astype(BF16)
    rows_ref[...] = jnp.zeros_like(rows_ref)
    norm = area
    for axis in range(3):
        value = geo_ref[axis : axis + 1, :]
        high = rounded(value)
        low = rounded(value - high)
        rows_ref[X + 2 * axis : X + 2 * axis + 1, :] = high
        rows_ref[X + 2 * axis + 1 : X + 2 * axis + 2, :] = low
        kept = high + low
        norm = norm + kept * kept
    for term in range(3):
        part = rounded(norm)
        rows_ref[NORM + term : NORM + term + 1, :] = part
        norm = norm - part
    high = rounded(area)
    rows_ref[AREA : AREA + 1, :] = high
    rows_ref[AREA + 1 : AREA + 2, :] = area - high
    rows_ref[MEMBER : MEMBER + 1, :] = conductor_ref[...].astype(F32).reshape(1, -1)
    rows_ref[ONE : ONE + 1, :] = jnp.ones_like(area)
    out_ref[rhs:, :] = rows_ref[...].astype(BF16)


def make_bundle(geometry, charges, conductor):
    rhs, panels = charges.shape
    return in_vmem(
        bundle_body,
        jax.ShapeDtypeStruct((rhs + FEATURES, panels), BF16),
        [pltpu.VMEM((FEATURES, panels), F32)],
    )(geometry, charges, conductor)


def left_side(features, table):
    return lax.dot_general(
        features, table, (((0,), (1,)), ((), ())), preferred_element_type=F32
    ).astype(BF16)


def right_side(features, table):
    return jnp.dot(table, features, preferred_element_type=F32).astype(BF16)


def tile_of(left, right):
    return lax.rsqrt(jnp.dot(left, right, preferred_element_type=F32)).astype(BF16)


def two_stage(steps, make, use, slots, width):
    strips = range(0, slots[0].shape[1], width)

    def one(step, now, later):
        carry = None
        for start in strips:
            if later is not None:
                later[:, start : start + width] = make(step + 1, start)
            carry = use(step, now[:, start : start + width], start, carry)
        use(step, None, None, carry)

    for start in strips:
        slots[0][:, start : start + width] = make(0, start)

    @pl.loop(0, steps // 2 - 1)
    def _(half):
        one(2 * half, slots[0], slots[1])
        one(2 * half + 1, slots[1], slots[0])

    one(steps - 2, slots[0], slots[1])
    one(steps - 1, slots[1], None)


def totals_of(field, bundle):
    rhs = field.shape[0]
    features = bundle[rhs:, :].astype(F32)
    area = features[AREA : AREA + 1, :] + features[AREA + 1 : AREA + 2, :]
    names = lax.broadcasted_iota(jnp.int32, field.shape, 0).astype(F32)
    member = jnp.where(names == features[MEMBER : MEMBER + 1, :], 1.0, 0.0).astype(BF16)
    scaled = field * area
    high = scaled.astype(BF16)
    low = (scaled - high.astype(F32)).astype(BF16)
    dims = (((1,), (1,)), ((), ()))
    return lax.dot_general(high, member, dims, preferred_element_type=F32) + lax.dot_general(
        low, member, dims, preferred_element_type=F32
    )


def self_body(
    rowblk, width, own_ref, ltab_ref, rtab_ref, index_ref, count_ref, odd_ref, out_ref, live_ref,
    left_ref, right_ref, *slots
):
    _, rhs, panels = out_ref.shape
    groups, near = index_ref.shape
    turn = jnp.where(odd_ref[0] == 1, 0, 2 * panels)
    slot = lax.broadcasted_iota(jnp.int32, (1, near), 1)
    for group in range(groups):
        index = index_ref[group : group + 1, :]
        moved = jnp.where(index < panels, index + turn, index)
        index = jnp.where(index >= 2 * panels, index - turn, moved)
        live_ref[group : group + 1, :] = jnp.where(slot < count_ref[group], index, -LANES)
    features = own_ref[rhs:, :]
    left_ref[...] = left_side(features, ltab_ref[...])
    right_ref[...] = right_side(features, rtab_ref[...])
    out_ref[...] = jnp.zeros_like(out_ref)

    def make(step, strip):
        start = pl.multiple_of(step * rowblk, rowblk)
        return tile_of(left_ref[pl.ds(start, rowblk), :], right_ref[:, strip : strip + width])

    def use(step, tile, strip, carry):
        if tile is None:
            return
        start = pl.multiple_of(step * rowblk, rowblk)
        out_ref[0, :, strip : strip + width] += jnp.dot(
            own_ref[0:rhs, pl.ds(start, rowblk)], tile, preferred_element_type=F32
        )

    two_stage(panels // rowblk, make, use, slots, width)


def self_field(own, tables, index, count, odd):
    rows, panels = own.shape
    rhs = rows - FEATURES
    rowblk, width = blocking(panels)
    vmem = pl.BlockSpec(memory_space=pltpu.VMEM)
    smem = pl.BlockSpec(memory_space=pltpu.SMEM)
    return pl.pallas_call(
        functools.partial(self_body, rowblk, width),
        out_shape=(
            jax.ShapeDtypeStruct((2, rhs, panels), F32),
            jax.ShapeDtypeStruct(index.shape, index.dtype),
        ),
        in_specs=[vmem] * 4 + [smem] * 2,
        out_specs=(vmem, vmem),
        scratch_shapes=[
            pltpu.VMEM((panels, DEPTH), BF16),
            pltpu.VMEM((DEPTH, panels), BF16),
            pltpu.VMEM((rowblk, panels), BF16),
            pltpu.VMEM((rowblk, panels), BF16),
        ],
        compiler_params=pltpu.CompilerParams(vmem_limit_bytes=VMEM_LIMIT),
        cost_estimate=pl.CostEstimate(flops=0, bytes_accessed=2**10, transcendentals=0),
    )(own, *tables, index, count, odd)


def pairs_body(
    rowblk, width, pair_ref, far_ref, ltab_ref, rtab_ref, field_in, totals_in,
    field_ref, back_ref, totals_ref, left_ref, right_ref, sum_ref, *slots
):
    blocks, rhs, panels = field_ref.shape
    for block in range(blocks):
        left_ref[block] = left_side(far_ref[block, rhs:, :], ltab_ref[...])
        right_ref[block] = right_side(pair_ref[block, rhs:, :], rtab_ref[...])
    field_ref[...] = field_in[...]
    sum_ref[...] = jnp.zeros_like(sum_ref)
    chunks = panels // rowblk

    def place(step):
        turn = step // chunks
        start = pl.multiple_of((step % chunks) * rowblk, rowblk)
        return turn // blocks, turn % blocks, start

    def make(step, strip):
        far, own, start = place(step)
        return tile_of(
            left_ref[far, pl.ds(start, rowblk), :], right_ref[own, :, strip : strip + width]
        )

    def use(step, tile, strip, carry):
        far, own, start = place(step)
        if tile is None:
            sum_ref[far, :, pl.ds(start, rowblk)] += carry
            return
        part = lax.dot_general(
            pair_ref[own, 0:rhs, strip : strip + width], tile, (((1,), (1,)), ((), ())),
            preferred_element_type=F32,
        )
        field_ref[own, :, strip : strip + width] += jnp.dot(
            far_ref[far, 0:rhs, pl.ds(start, rowblk)], tile, preferred_element_type=F32
        )
        return part if carry is None else carry + part

    two_stage(blocks * blocks * chunks, make, use, slots, width)
    totals = totals_in[...]
    for block in range(blocks):
        totals = totals + totals_of(sum_ref[block], far_ref[block])
    totals_ref[...] = totals
    back_ref[...] = sum_ref[...].astype(BF16)


def pairs_field(pair, far, tables, field, totals, last):
    blocks, rows, panels = pair.shape
    rhs = rows - FEATURES
    rowblk, width = blocking(panels)
    work = 800 * panels * panels * blocks * blocks
    return in_vmem(
        functools.partial(pairs_body, rowblk, width),
        (
            jax.ShapeDtypeStruct((blocks, rhs, panels), F32),
            jax.ShapeDtypeStruct((blocks, rhs, panels), BF16),
            jax.ShapeDtypeStruct(totals.shape, F32),
        ),
        [
            pltpu.VMEM((blocks, panels, DEPTH), BF16),
            pltpu.VMEM((blocks, DEPTH, panels), BF16),
            pltpu.VMEM((blocks, rhs, panels), F32),
            pltpu.VMEM((rowblk, panels), BF16),
            pltpu.VMEM((rowblk, panels), BF16),
        ],
        flops=work if last else 0,
    )(pair, far, *tables, field, totals)


def near_body(
    together, twin_ref, own_ref, other_ref, index_ref, weight_ref, field_in, totals_in,
    pair_ref, field_ref, totals_ref, ext_ref
):
    rhs, panels = own_ref.shape
    groups, near = index_ref.shape
    pieces = panels // LANES
    for side, ref in enumerate((twin_ref, own_ref, other_ref)):
        for piece in range(pieces):
            start = rhs * (side * pieces + piece)
            ext_ref[start : start + rhs, :] = ref[:, piece * LANES : (piece + 1) * LANES]
    field_ref[...] = field_in[...]

    @pl.loop(0, groups // together)
    def _(batch):
        rows = [batch * together + member for member in range(together)]
        index = jnp.concatenate([index_ref[pl.ds(group, 1), :] for group in rows], axis=1)
        lane = index & (LANES - 1)
        place = jnp.broadcast_to(index >> (LANES.bit_length() - 1), (rhs, together * near))
        names = lax.broadcasted_iota(jnp.int32, (LANES, together * near), 0)
        pick = jnp.where(names == lane, 1.0, 0.0).astype(BF16)
        taken = jnp.zeros((rhs, together * near), F32)
        found = jnp.dot(ext_ref[...], pick, preferred_element_type=F32)
        for piece in range(3 * pieces):
            part = found[piece * rhs : (piece + 1) * rhs, :]
            taken = jnp.where(place == piece, part, taken)
        taken = taken.astype(BF16)
        width = weight_ref.shape[1]
        for member, group in enumerate(rows):
            field_ref[0, :, pl.ds(pl.multiple_of(group * width, width), width)] += lax.dot_general(
                taken[:, member * near : (member + 1) * near], weight_ref[group],
                (((1,), (1,)), ((), ())), preferred_element_type=F32,
            )

    totals = totals_in[...]
    for block in range(field_ref.shape[0]):
        totals = totals + totals_of(field_ref[block], pair_ref[block])
    height = totals_ref.shape[1]
    flat = jnp.concatenate([totals[r : r + height, :] for r in range(0, rhs, height)], axis=1)
    totals_ref[...] = jnp.broadcast_to(flat[None], totals_ref.shape)


def near_field(twin, own, other, index, weight, field, totals, pair):
    rhs, panels = own.shape
    vmem = pl.BlockSpec(memory_space=pltpu.VMEM)
    together = next(n for n in (4, 2, 1) if index.shape[0] % n == 0)
    return pl.pallas_call(
        functools.partial(near_body, together),
        out_shape=(
            jax.ShapeDtypeStruct(field.shape, F32),
            jax.ShapeDtypeStruct((lax.axis_size(AXES), rhs * rhs // 128, 128), F32),
        ),
        in_specs=[vmem] * 8,
        out_specs=(vmem, vmem),
        scratch_shapes=[pltpu.VMEM((3 * panels // LANES * rhs, LANES), BF16)],
        compiler_params=pltpu.CompilerParams(vmem_limit_bytes=VMEM_LIMIT),
        cost_estimate=pl.CostEstimate(flops=4 * 10**9, bytes_accessed=2**10, transcendentals=0),
    )(twin, own, other, index, weight, field, totals, pair)


def finish_body(field_ref, part_ref, totals_ref, potential_out, totals_out):
    potential_out[...] = field_ref[0] + part_ref[...].astype(F32)
    total = jnp.sum(totals_ref[...], axis=0)
    rhs, height = totals_out.shape[0], total.shape[0]
    for turn in range(rhs // height):
        totals_out[turn * height : (turn + 1) * height, :] = total[:, turn * rhs : (turn + 1) * rhs]


def send(value, source_of):
    count = lax.axis_size(AXES)
    return lax.ppermute(value, AXES, [(source_of(d), d) for d in range(count)])


def send_back(value, source_of):
    count = lax.axis_size(AXES)
    return lax.ppermute(value, AXES, [(d, source_of(d)) for d in range(count)])


def paired_blocks(geometry, charges, near_index, near_count, near_weight, conductor):
    cols = lax.axis_size("col")
    core, flip_x, far_z = cols, 2 * cols, cols // 2
    rhs = charges.shape[0]

    def partner(d, far):
        second = bool(d & core)
        mask = 1 + (flip_x if bool(d & 1) != second else 0) + (2 if second else 0)
        return d ^ (mask + (far_z if far else 0))

    def other_neighbour(d):
        count = lax.axis_size(AXES)
        return (d + (1 if d & 1 else -1)) % count

    tables = (chooser(True), chooser(False))
    bundle = make_bundle(geometry, charges, conductor)
    sibling = send(bundle, lambda d: d ^ core)
    pair = jnp.stack([bundle, sibling])
    close = send(pair, lambda d: partner(d, False))
    odd = (lax.axis_index(AXES) % 2).reshape(1)
    field, live = self_field(bundle, tables, near_index, near_count, odd)
    late_pair, field = lax.optimization_barrier((pair, field))
    far = send(late_pair, lambda d: partner(d, True))
    totals = jnp.zeros((rhs, rhs), F32)
    field, close_back, totals = pairs_field(pair, close, tables, field, totals, False)
    close_back = send_back(close_back, lambda d: partner(d, False))
    late_charges, field = lax.optimization_barrier((charges, field))
    twin = send(late_charges, lambda d: d ^ 1)
    other = send(late_charges, other_neighbour)
    field, far_back, totals = pairs_field(pair, far, tables, field, totals, True)
    far_back = send_back(far_back, lambda d: partner(d, True))
    field, totals = near_field(
        twin, charges, other, live, near_weight, field, totals, pair
    )
    close_back, totals = lax.optimization_barrier((close_back, totals))
    totals = lax.all_to_all(totals, AXES, 0, 0, tiled=True)
    field = field + close_back.astype(F32) + far_back.astype(F32)
    twin_part = send(field[1].astype(BF16), lambda d: d ^ core)
    return in_vmem(
        finish_body,
        (jax.ShapeDtypeStruct(charges.shape, F32), jax.ShapeDtypeStruct((rhs, rhs), F32)),
    )(field, twin_part, totals)


def passed_along(value, axis, steps):
    count = lax.axis_size(axis)
    pairs = [(source, (source + steps) % count) for source in range(count)]
    return lax.ppermute(value, axis, pairs)


def extended_2(x, sides, width):
    for axis, dim in sides:
        count, length = (lax.axis_size(axis), x.shape[dim])
        up = [(i, (i + 1) % count) for i in range(count)]
        down = [(j, i) for i, j in up]
        last = lax.slice_in_dim(x, length - width, length, axis=dim)
        initial = lax.slice_in_dim(x, 0, width, axis=dim)
        before = lax.ppermute(last, axis, up)
        after = lax.ppermute(initial, axis, down)
        x = jnp.concatenate([before, x, after], axis=dim)
    return x


def kernel_tile(rows, cols):
    delta_x = rows[0][:, None] - cols[0][None, :]
    delta_y = rows[1][:, None] - cols[1][None, :]
    delta_z = rows[2][:, None] - cols[2][None, :]
    spread = rows[3][:, None] * rows[3][:, None] + cols[3][None, :] * cols[3][None, :]
    squared = delta_x * delta_x + delta_y * delta_y + delta_z * delta_z + spread
    return lax.rsqrt(squared).astype(BF16)


def pair_products(own_geo, own_w, other_geo, other_w, backwards):
    panels = own_geo.shape[1]
    rowblk = min(256, panels)
    pieces = []
    back = jnp.zeros(other_w.shape, F32)
    for start in range(0, panels, rowblk):
        tile = kernel_tile(own_geo[:, start : start + rowblk], other_geo)
        pieces.append(
            lax.dot_general(
                other_w, tile, (((1,), (1,)), ((), ())), preferred_element_type=F32
            )
        )
        if backwards:
            back = back + jnp.dot(
                own_w[:, start : start + rowblk], tile, preferred_element_type=F32
            )
    return (jnp.concatenate(pieces, axis=1), back)


def from_lower(geometry, weighted, offset):
    geo = passed_along(geometry, ("row", "col"), offset)
    wts = passed_along(weighted, ("row", "col"), offset)
    return (geo, wts)


def give_back(partial_value, offset):
    return passed_along(partial_value, ("row", "col"), -offset)


def offset_rounds(geometry, charges, near_index, near_count, near_weight, conductor):
    devices = lax.axis_size(("row", "col"))
    stride = devices // (2 * ROUNDS)
    offsets = [1 + k * stride for k in range(ROUNDS)]
    panels = charges.shape[1]
    groups_dev = near_index.shape[0]
    area = geometry[3] * geometry[3]
    weighted = (charges.astype(F32) * area[None, :]).astype(BF16)
    field, unused = pair_products(geometry, weighted, geometry, weighted, False)
    for turn in range(ROUNDS):
        offset = offsets[turn]
        lower_geo, lower_w = from_lower(geometry, weighted, offset)
        forward, back = pair_products(geometry, weighted, lower_geo, lower_w, True)
        field = field + forward + give_back(back.astype(BF16), offset).astype(F32)
    extended = extended_2(charges, ((("row", "col"), 1),), panels)
    gathered = jnp.take(extended, near_index.reshape(-1), axis=1).reshape(
        charges.shape[0], groups_dev, near_index.shape[1]
    )
    live = jnp.arange(near_index.shape[1], dtype=jnp.int32)[None, :] < near_count[:, None]
    gathered = jnp.where(live[None], gathered, jnp.zeros_like(gathered))
    correction = jnp.einsum(
        "rgk,gtk->rgt", gathered, near_weight, preferred_element_type=F32
    )
    field = field + correction.reshape(charges.shape[0], panels)
    member = (conductor[:, None] == jnp.arange(charges.shape[0], dtype=jnp.int32)[None, :]).astype(
        F32
    )
    local_totals = jnp.dot(
        field * area[None, :],
        member,
        precision=lax.Precision.HIGHEST,
        preferred_element_type=F32,
    )
    totals = lax.psum(local_totals, ("row", "col"))
    return (field, totals)


def on_device(geometry, *rest):
    if lax.axis_size(AXES) == 4 * ROUNDS:
        return paired_blocks(geometry, *rest)
    return offset_rounds(geometry, *rest)


def solution(mesh):
    in_specs = (
        P(None, ("row", "col")),
        P(None, ("row", "col")),
        P(("row", "col"), None),
        P(("row", "col")),
        P(("row", "col"), None, None),
        P(("row", "col")),
    )
    out_specs = (P(None, ("row", "col")), P())
    return jax.shard_map(
        on_device, mesh=mesh, in_specs=in_specs, out_specs=out_specs, check_vma=False
    )
```

```python
import functools

import jax
import jax.numpy as jnp
import numpy as np
from jax import lax
from jax.experimental import pallas as pl
from jax.experimental.pallas import tpu as pltpu
from jax.sharding import PartitionSpec as P

ROUNDS = 8
AXES = ("row", "col")
F32 = jnp.float32
BF16 = jnp.bfloat16

X, AREA, MEMBER = 0, 6, 7
FEATURES = 8
NORM, ONE = 8, 11
TERMS = 16
LANES = 128
DEPTH = 32
VMEM_LIMIT = 48 * 2**20


def chooser(left):
    table = np.zeros((DEPTH, TERMS), np.float32)
    row = 0
    for axis in range(3):
        for first in range(2):
            for second in range(2):
                feature = X + 2 * axis + (first if left else second)
                table[row, feature] = 1.0 if left else -2.0
                row += 1
    for term in range(3):
        table[row, NORM + term if left else ONE] = 1.0
        table[row + 3, ONE if left else NORM + term] = 1.0
        row += 1
    return jnp.asarray(table, BF16)


def blocking(panels):
    rows = next((r for r in (384, 256, 128) if panels % (2 * r) == 0), panels // 2)
    return rows, 256 if panels % 256 == 0 else panels


def in_vmem(body, out_shape, scratch=(), flops=0):
    return pl.pallas_call(
        body,
        out_shape=out_shape,
        scratch_shapes=list(scratch),
        compiler_params=pltpu.CompilerParams(vmem_limit_bytes=VMEM_LIMIT),
        cost_estimate=pl.CostEstimate(flops=flops, bytes_accessed=2**10, transcendentals=0),
    )


def rounded(value):
    return value.astype(BF16).astype(F32)


def bundle_body(geo_ref, charges_ref, conductor_ref, out_ref, rows_ref):
    rhs = charges_ref.shape[0]
    size = geo_ref[3:4, :]
    area = size * size
    rows_ref[0:rhs, :] = charges_ref[...].astype(F32) * area
    for axis in range(3):
        value = geo_ref[axis : axis + 1, :]
        high = rounded(value)
        row = rhs + X + 2 * axis
        rows_ref[row : row + 1, :] = high
        rows_ref[row + 1 : row + 2, :] = value - high
    rows_ref[rhs + AREA : rhs + AREA + 1, :] = area
    rows_ref[rhs + MEMBER : rhs + MEMBER + 1, :] = conductor_ref[...].astype(F32).reshape(1, -1)
    out_ref[...] = rows_ref[...].astype(BF16)


def features_of(bundle):
    rows = bundle.shape[0]
    return bundle.astype(F32)[rows - FEATURES :, :]


def write_terms(features, terms_ref):
    norm = features[AREA : AREA + 1, :]
    for axis in range(3):
        row = X + 2 * axis
        kept = features[row : row + 1, :] + features[row + 1 : row + 2, :]
        norm = norm + kept * kept
    terms_ref[0:FEATURES, :] = features
    terms_ref[NORM:, :] = jnp.zeros((TERMS - NORM, norm.shape[1]), F32)
    for term in range(3):
        part = rounded(norm)
        terms_ref[NORM + term : NORM + term + 1, :] = part
        norm = norm - part
    terms_ref[ONE : ONE + 1, :] = jnp.ones_like(norm)


def make_bundle(geometry, charges, conductor):
    rhs, panels = charges.shape
    return in_vmem(
        bundle_body,
        jax.ShapeDtypeStruct((rhs + FEATURES, panels), BF16),
        [pltpu.VMEM((rhs + FEATURES, panels), F32)],
    )(geometry, charges, conductor)


def left_side(terms_ref, table):
    return lax.dot_general(
        terms_ref[...].astype(BF16), table, (((0,), (1,)), ((), ())), preferred_element_type=F32
    ).astype(BF16)


def right_side(terms_ref, table):
    return jnp.dot(table, terms_ref[...].astype(BF16), preferred_element_type=F32).astype(BF16)


def tile_of(left, right):
    return lax.rsqrt(jnp.dot(left, right, preferred_element_type=F32)).astype(BF16)


def two_stage(steps, make, use, slots, width):
    strips = range(0, slots[0].shape[1], width)

    def one(step, now, later):
        carry = None
        for start in strips:
            if later is not None:
                later[:, start : start + width] = make(step + 1, start)
            carry = use(step, now[:, start : start + width], start, carry)
        use(step, None, None, carry)

    for start in strips:
        slots[0][:, start : start + width] = make(0, start)

    @pl.loop(0, steps // 2 - 1)
    def _(half):
        one(2 * half, slots[0], slots[1])
        one(2 * half + 1, slots[1], slots[0])

    one(steps - 2, slots[0], slots[1])
    one(steps - 1, slots[1], None)


def totals_of(field, bundle):
    rhs = field.shape[0]
    features = features_of(bundle)
    area = features[AREA : AREA + 1, :]
    names = lax.broadcasted_iota(jnp.int32, field.shape, 0).astype(F32)
    member = jnp.where(names == features[MEMBER : MEMBER + 1, :], 1.0, 0.0).astype(BF16)
    scaled = field * area
    high = scaled.astype(BF16)
    low = (scaled - high.astype(F32)).astype(BF16)
    dims = (((1,), (1,)), ((), ()))
    return lax.dot_general(high, member, dims, preferred_element_type=F32) + lax.dot_general(
        low, member, dims, preferred_element_type=F32
    )


def self_body(
    rowblk, width, own_ref, ltab_ref, rtab_ref, index_ref, count_ref, odd_ref, out_ref, live_ref,
    left_ref, right_ref, terms_ref, *slots
):
    _, rhs, panels = out_ref.shape
    groups, near = index_ref.shape
    turn = jnp.where(odd_ref[0] == 1, 0, 2 * panels)
    slot = lax.broadcasted_iota(jnp.int32, (1, near), 1)
    for group in range(groups):
        index = index_ref[group : group + 1, :]
        moved = jnp.where(index < panels, index + turn, index)
        index = jnp.where(index >= 2 * panels, index - turn, moved)
        live_ref[group : group + 1, :] = jnp.where(slot < count_ref[group], index, -LANES)
    write_terms(features_of(own_ref[...]), terms_ref)
    left_ref[...] = left_side(terms_ref, ltab_ref[...])
    right_ref[...] = right_side(terms_ref, rtab_ref[...])
    out_ref[...] = jnp.zeros_like(out_ref)

    def make(step, strip):
        start = pl.multiple_of(step * rowblk, rowblk)
        return tile_of(left_ref[pl.ds(start, rowblk), :], right_ref[:, strip : strip + width])

    def use(step, tile, strip, carry):
        if tile is None:
            return
        start = pl.multiple_of(step * rowblk, rowblk)
        out_ref[0, :, strip : strip + width] += jnp.dot(
            own_ref[0:rhs, pl.ds(start, rowblk)], tile, preferred_element_type=F32
        )

    two_stage(panels // rowblk, make, use, slots, width)


def self_field(own, tables, index, count, odd):
    rows, panels = own.shape
    rhs = rows - FEATURES
    rowblk, width = blocking(panels)
    vmem = pl.BlockSpec(memory_space=pltpu.VMEM)
    smem = pl.BlockSpec(memory_space=pltpu.SMEM)
    return pl.pallas_call(
        functools.partial(self_body, rowblk, width),
        out_shape=(
            jax.ShapeDtypeStruct((2, rhs, panels), F32),
            jax.ShapeDtypeStruct(index.shape, index.dtype),
        ),
        in_specs=[vmem] * 4 + [smem] * 2,
        out_specs=(vmem, vmem),
        scratch_shapes=[
            pltpu.VMEM((panels, DEPTH), BF16),
            pltpu.VMEM((DEPTH, panels), BF16),
            pltpu.VMEM((TERMS, panels), F32),
            pltpu.VMEM((rowblk, panels), BF16),
            pltpu.VMEM((rowblk, panels), BF16),
        ],
        compiler_params=pltpu.CompilerParams(vmem_limit_bytes=VMEM_LIMIT),
        cost_estimate=pl.CostEstimate(flops=0, bytes_accessed=2**10, transcendentals=0),
    )(own, *tables, index, count, odd)


def pairs_body(
    rowblk, width, pair_ref, far_ref, ltab_ref, rtab_ref, field_in, totals_in,
    field_ref, back_ref, totals_ref, left_ref, right_ref, terms_ref, sum_ref, *slots
):
    blocks, rhs, panels = field_ref.shape
    for block in range(blocks):
        write_terms(features_of(far_ref[block]), terms_ref)
        left_ref[block] = left_side(terms_ref, ltab_ref[...])
        write_terms(features_of(pair_ref[block]), terms_ref)
        right_ref[block] = right_side(terms_ref, rtab_ref[...])
    field_ref[...] = field_in[...]
    sum_ref[...] = jnp.zeros_like(sum_ref)
    chunks = panels // rowblk

    def place(step):
        turn = step // chunks
        start = pl.multiple_of((step % chunks) * rowblk, rowblk)
        return turn // blocks, turn % blocks, start

    def make(step, strip):
        far, own, start = place(step)
        return tile_of(
            left_ref[far, pl.ds(start, rowblk), :], right_ref[own, :, strip : strip + width]
        )

    def use(step, tile, strip, carry):
        far, own, start = place(step)
        if tile is None:
            sum_ref[far, :, pl.ds(start, rowblk)] += carry
            return
        part = lax.dot_general(
            pair_ref[own, 0:rhs, strip : strip + width], tile, (((1,), (1,)), ((), ())),
            preferred_element_type=F32,
        )
        field_ref[own, :, strip : strip + width] += jnp.dot(
            far_ref[far, 0:rhs, pl.ds(start, rowblk)], tile, preferred_element_type=F32
        )
        return part if carry is None else carry + part

    two_stage(blocks * blocks * chunks, make, use, slots, width)
    totals = totals_in[...]
    for block in range(blocks):
        totals = totals + totals_of(sum_ref[block], far_ref[block])
    totals_ref[...] = totals
    back_ref[...] = sum_ref[...].astype(BF16)


def pairs_field(pair, far, tables, field, totals, last):
    blocks, rows, panels = pair.shape
    rhs = rows - FEATURES
    rowblk, width = blocking(panels)
    work = 3200 * panels * panels * blocks * blocks
    return in_vmem(
        functools.partial(pairs_body, rowblk, width),
        (
            jax.ShapeDtypeStruct((blocks, rhs, panels), F32),
            jax.ShapeDtypeStruct((blocks, rhs, panels), BF16),
            jax.ShapeDtypeStruct(totals.shape, F32),
        ),
        [
            pltpu.VMEM((blocks, panels, DEPTH), BF16),
            pltpu.VMEM((blocks, DEPTH, panels), BF16),
            pltpu.VMEM((TERMS, panels), F32),
            pltpu.VMEM((blocks, rhs, panels), F32),
            pltpu.VMEM((rowblk, panels), BF16),
            pltpu.VMEM((rowblk, panels), BF16),
        ],
        flops=work if last else 0,
    )(pair, far, *tables, field, totals)


def near_body(
    together, twin_ref, own_ref, other_ref, index_ref, weight_ref, field_in, totals_in,
    pair_ref, field_ref, totals_ref, ext_ref
):
    rhs, panels = own_ref.shape
    groups, near = index_ref.shape
    pieces = panels // LANES
    for side, ref in enumerate((twin_ref, own_ref, other_ref)):
        for piece in range(pieces):
            start = rhs * (side * pieces + piece)
            ext_ref[start : start + rhs, :] = ref[:, piece * LANES : (piece + 1) * LANES]
    field_ref[...] = field_in[...]

    @pl.loop(0, groups // together)
    def _(batch):
        rows = [batch * together + member for member in range(together)]
        index = jnp.concatenate([index_ref[pl.ds(group, 1), :] for group in rows], axis=1)
        lane = index & (LANES - 1)
        place = jnp.broadcast_to(index >> (LANES.bit_length() - 1), (rhs, together * near))
        names = lax.broadcasted_iota(jnp.int32, (LANES, together * near), 0)
        pick = jnp.where(names == lane, 1.0, 0.0).astype(BF16)
        taken = jnp.zeros((rhs, together * near), F32)
        found = jnp.dot(ext_ref[...], pick, preferred_element_type=F32)
        for piece in range(3 * pieces):
            part = found[piece * rhs : (piece + 1) * rhs, :]
            taken = jnp.where(place == piece, part, taken)
        taken = taken.astype(BF16)
        width = weight_ref.shape[1]
        for member, group in enumerate(rows):
            field_ref[0, :, pl.ds(pl.multiple_of(group * width, width), width)] += lax.dot_general(
                taken[:, member * near : (member + 1) * near], weight_ref[group],
                (((1,), (1,)), ((), ())), preferred_element_type=F32,
            )

    totals = totals_in[...]
    for block in range(field_ref.shape[0]):
        totals = totals + totals_of(field_ref[block], pair_ref[block])
    height = totals_ref.shape[1]
    flat = jnp.concatenate([totals[r : r + height, :] for r in range(0, rhs, height)], axis=1)
    totals_ref[...] = jnp.broadcast_to(flat[None], totals_ref.shape)


def near_field(twin, own, other, index, weight, field, totals, pair):
    rhs, panels = own.shape
    vmem = pl.BlockSpec(memory_space=pltpu.VMEM)
    together = next(n for n in (4, 2, 1) if index.shape[0] % n == 0)
    return pl.pallas_call(
        functools.partial(near_body, together),
        out_shape=(
            jax.ShapeDtypeStruct(field.shape, F32),
            jax.ShapeDtypeStruct((lax.axis_size(AXES), rhs * rhs // 128, 128), F32),
        ),
        in_specs=[vmem] * 8,
        out_specs=(vmem, vmem),
        scratch_shapes=[pltpu.VMEM((3 * panels // LANES * rhs, LANES), BF16)],
        compiler_params=pltpu.CompilerParams(vmem_limit_bytes=VMEM_LIMIT),
        cost_estimate=pl.CostEstimate(flops=2 * 10**9, bytes_accessed=2**10, transcendentals=0),
    )(twin, own, other, index, weight, field, totals, pair)


def finish_body(field_ref, part_ref, totals_ref, potential_out, totals_out):
    potential_out[...] = field_ref[0] + part_ref[...].astype(F32)
    total = jnp.sum(totals_ref[...], axis=0)
    rhs, height = totals_out.shape[0], total.shape[0]
    for turn in range(rhs // height):
        totals_out[turn * height : (turn + 1) * height, :] = total[:, turn * rhs : (turn + 1) * rhs]


def send(value, source_of):
    count = lax.axis_size(AXES)
    return lax.ppermute(value, AXES, [(source_of(d), d) for d in range(count)])


def send_back(value, source_of):
    count = lax.axis_size(AXES)
    return lax.ppermute(value, AXES, [(d, source_of(d)) for d in range(count)])


def paired_blocks(geometry, charges, near_index, near_count, near_weight, conductor):
    cols = lax.axis_size("col")
    core, flip_x, far_z = cols, 2 * cols, cols // 2
    rhs = charges.shape[0]

    def partner(d, far):
        second = bool(d & core)
        mask = 1 + (flip_x if bool(d & 1) != second else 0) + (2 if second else 0)
        return d ^ (mask + (far_z if far else 0))

    def other_neighbour(d):
        count = lax.axis_size(AXES)
        return (d + (1 if d & 1 else -1)) % count

    tables = (chooser(True), chooser(False))
    bundle = make_bundle(geometry, charges, conductor)
    sibling = send(bundle, lambda d: d ^ core)
    pair = jnp.stack([bundle, sibling])
    close = send(pair, lambda d: partner(d, False))
    odd = (lax.axis_index(AXES) % 2).reshape(1)
    field, live = self_field(bundle, tables, near_index, near_count, odd)
    late_pair, field = lax.optimization_barrier((pair, field))
    far = send(late_pair, lambda d: partner(d, True))
    totals = jnp.zeros((rhs, rhs), F32)
    field, close_back, totals = pairs_field(pair, close, tables, field, totals, False)
    close_back = send_back(close_back, lambda d: partner(d, False))
    late_charges, field = lax.optimization_barrier((charges, field))
    twin = send(late_charges, lambda d: d ^ 1)
    other = send(late_charges, other_neighbour)
    field, far_back, totals = pairs_field(pair, far, tables, field, totals, True)
    far_back = send_back(far_back, lambda d: partner(d, True))
    field, totals = near_field(
        twin, charges, other, live, near_weight, field, totals, pair
    )
    close_back, totals = lax.optimization_barrier((close_back, totals))
    totals = lax.all_to_all(totals, AXES, 0, 0, tiled=True)
    field = field + close_back.astype(F32) + far_back.astype(F32)
    twin_part = send(field[1].astype(BF16), lambda d: d ^ core)
    return in_vmem(
        finish_body,
        (jax.ShapeDtypeStruct(charges.shape, F32), jax.ShapeDtypeStruct((rhs, rhs), F32)),
    )(field, twin_part, totals)


def passed_along(value, axis, steps):
    count = lax.axis_size(axis)
    pairs = [(source, (source + steps) % count) for source in range(count)]
    return lax.ppermute(value, axis, pairs)


def extended_2(x, sides, width):
    for axis, dim in sides:
        count, length = (lax.axis_size(axis), x.shape[dim])
        up = [(i, (i + 1) % count) for i in range(count)]
        down = [(j, i) for i, j in up]
        last = lax.slice_in_dim(x, length - width, length, axis=dim)
        initial = lax.slice_in_dim(x, 0, width, axis=dim)
        before = lax.ppermute(last, axis, up)
        after = lax.ppermute(initial, axis, down)
        x = jnp.concatenate([before, x, after], axis=dim)
    return x


def kernel_tile(rows, cols):
    delta_x = rows[0][:, None] - cols[0][None, :]
    delta_y = rows[1][:, None] - cols[1][None, :]
    delta_z = rows[2][:, None] - cols[2][None, :]
    spread = rows[3][:, None] * rows[3][:, None] + cols[3][None, :] * cols[3][None, :]
    squared = delta_x * delta_x + delta_y * delta_y + delta_z * delta_z + spread
    return lax.rsqrt(squared).astype(BF16)


def pair_products(own_geo, own_w, other_geo, other_w, backwards):
    panels = own_geo.shape[1]
    rowblk = min(256, panels)
    pieces = []
    back = jnp.zeros(other_w.shape, F32)
    for start in range(0, panels, rowblk):
        tile = kernel_tile(own_geo[:, start : start + rowblk], other_geo)
        pieces.append(
            lax.dot_general(
                other_w, tile, (((1,), (1,)), ((), ())), preferred_element_type=F32
            )
        )
        if backwards:
            back = back + jnp.dot(
                own_w[:, start : start + rowblk], tile, preferred_element_type=F32
            )
    return (jnp.concatenate(pieces, axis=1), back)


def from_lower(geometry, weighted, offset):
    geo = passed_along(geometry, ("row", "col"), offset)
    wts = passed_along(weighted, ("row", "col"), offset)
    return (geo, wts)


def give_back(partial_value, offset):
    return passed_along(partial_value, ("row", "col"), -offset)


def offset_rounds(geometry, charges, near_index, near_count, near_weight, conductor):
    devices = lax.axis_size(("row", "col"))
    stride = devices // (2 * ROUNDS)
    offsets = [1 + k * stride for k in range(ROUNDS)]
    panels = charges.shape[1]
    groups_dev = near_index.shape[0]
    area = geometry[3] * geometry[3]
    weighted = (charges.astype(F32) * area[None, :]).astype(BF16)
    field, unused = pair_products(geometry, weighted, geometry, weighted, False)
    for turn in range(ROUNDS):
        offset = offsets[turn]
        lower_geo, lower_w = from_lower(geometry, weighted, offset)
        forward, back = pair_products(geometry, weighted, lower_geo, lower_w, True)
        field = field + forward + give_back(back.astype(BF16), offset).astype(F32)
    extended = extended_2(charges, ((("row", "col"), 1),), panels)
    gathered = jnp.take(extended, near_index.reshape(-1), axis=1).reshape(
        charges.shape[0], groups_dev, near_index.shape[1]
    )
    live = jnp.arange(near_index.shape[1], dtype=jnp.int32)[None, :] < near_count[:, None]
    gathered = jnp.where(live[None], gathered, jnp.zeros_like(gathered))
    correction = jnp.einsum(
        "rgk,gtk->rgt", gathered, near_weight, preferred_element_type=F32
    )
    field = field + correction.reshape(charges.shape[0], panels)
    member = (conductor[:, None] == jnp.arange(charges.shape[0], dtype=jnp.int32)[None, :]).astype(
        F32
    )
    local_totals = jnp.dot(
        field * area[None, :],
        member,
        precision=lax.Precision.HIGHEST,
        preferred_element_type=F32,
    )
    totals = lax.psum(local_totals, ("row", "col"))
    return (field, totals)


def on_device(geometry, *rest):
    if lax.axis_size(AXES) == 4 * ROUNDS:
        return paired_blocks(geometry, *rest)
    return offset_rounds(geometry, *rest)


def solution(mesh):
    in_specs = (
        P(None, ("row", "col")),
        P(None, ("row", "col")),
        P(("row", "col"), None),
        P(("row", "col")),
        P(("row", "col"), None, None),
        P(("row", "col")),
    )
    out_specs = (P(None, ("row", "col")), P())
    return jax.shard_map(
        on_device, mesh=mesh, in_specs=in_specs, out_specs=out_specs, check_vma=False
    )
```

```python
import functools

import jax
import jax.numpy as jnp
import numpy as np
from jax import lax
from jax.experimental import pallas as pl
from jax.experimental.pallas import tpu as pltpu
from jax.sharding import PartitionSpec as P

ROUNDS = 8
AXES = ("row", "col")
F32 = jnp.float32
BF16 = jnp.bfloat16

X, AREA, MEMBER = 0, 6, 7
FEATURES = 8
NORM, ONE = 8, 11
TERMS = 16
LANES = 128
DEPTH = 32
VMEM_LIMIT = 48 * 2**20


def chooser(left):
    table = np.zeros((DEPTH, TERMS), np.float32)
    row = 0
    for axis in range(3):
        for first in range(2):
            for second in range(2):
                feature = X + 2 * axis + (first if left else second)
                table[row, feature] = 1.0 if left else -2.0
                row += 1
    for term in range(3):
        table[row, NORM + term if left else ONE] = 1.0
        table[row + 3, ONE if left else NORM + term] = 1.0
        row += 1
    return jnp.asarray(table, BF16)


def blocking(panels):
    rows = next((r for r in (384, 256, 128) if panels % (2 * r) == 0), panels // 2)
    return rows, 256 if panels % 256 == 0 else panels


def in_vmem(body, out_shape, scratch=(), flops=0):
    return pl.pallas_call(
        body,
        out_shape=out_shape,
        scratch_shapes=list(scratch),
        compiler_params=pltpu.CompilerParams(vmem_limit_bytes=VMEM_LIMIT),
        cost_estimate=pl.CostEstimate(flops=flops, bytes_accessed=2**10, transcendentals=0),
    )


def rounded(value):
    return value.astype(BF16).astype(F32)


def bundle_body(geo_ref, charges_ref, conductor_ref, out_ref, rows_ref):
    rhs = charges_ref.shape[0]
    size = geo_ref[3:4, :]
    area = size * size
    rows_ref[0:rhs, :] = charges_ref[...].astype(F32) * area
    for axis in range(3):
        value = geo_ref[axis : axis + 1, :]
        high = rounded(value)
        row = rhs + X + 2 * axis
        rows_ref[row : row + 1, :] = high
        rows_ref[row + 1 : row + 2, :] = value - high
    rows_ref[rhs + AREA : rhs + AREA + 1, :] = area
    rows_ref[rhs + MEMBER : rhs + MEMBER + 1, :] = conductor_ref[...].astype(F32).reshape(1, -1)
    out_ref[...] = rows_ref[...].astype(BF16)


def features_of(bundle):
    rows = bundle.shape[0]
    return bundle.astype(F32)[rows - FEATURES :, :]


def write_terms(features, terms_ref):
    norm = features[AREA : AREA + 1, :]
    for axis in range(3):
        row = X + 2 * axis
        kept = features[row : row + 1, :] + features[row + 1 : row + 2, :]
        norm = norm + kept * kept
    terms_ref[0:FEATURES, :] = features
    terms_ref[NORM:, :] = jnp.zeros((TERMS - NORM, norm.shape[1]), F32)
    for term in range(3):
        part = rounded(norm)
        terms_ref[NORM + term : NORM + term + 1, :] = part
        norm = norm - part
    terms_ref[ONE : ONE + 1, :] = jnp.ones_like(norm)


def make_bundle(geometry, charges, conductor):
    rhs, panels = charges.shape
    return in_vmem(
        bundle_body,
        jax.ShapeDtypeStruct((rhs + FEATURES, panels), BF16),
        [pltpu.VMEM((rhs + FEATURES, panels), F32)],
    )(geometry, charges, conductor)


def left_side(terms_ref, table):
    return lax.dot_general(
        terms_ref[...].astype(BF16), table, (((0,), (1,)), ((), ())), preferred_element_type=F32
    ).astype(BF16)


def right_side(terms_ref, table):
    return jnp.dot(table, terms_ref[...].astype(BF16), preferred_element_type=F32).astype(BF16)


def tile_of(left, right):
    return lax.rsqrt(jnp.dot(left, right, preferred_element_type=F32)).astype(BF16)


def two_stage(steps, make, use, slots, width):
    strips = range(0, slots[0].shape[1], width)

    def one(step, now, later):
        carry = None
        for start in strips:
            if later is not None:
                later[:, start : start + width] = make(step + 1, start)
            carry = use(step, now[:, start : start + width], start, carry)
        use(step, None, None, carry)

    for start in strips:
        slots[0][:, start : start + width] = make(0, start)

    @pl.loop(0, steps // 2 - 1)
    def _(half):
        one(2 * half, slots[0], slots[1])
        one(2 * half + 1, slots[1], slots[0])

    one(steps - 2, slots[0], slots[1])
    one(steps - 1, slots[1], None)


def totals_of(field, bundle):
    rhs = field.shape[0]
    features = features_of(bundle)
    area = features[AREA : AREA + 1, :]
    names = lax.broadcasted_iota(jnp.int32, field.shape, 0).astype(F32)
    member = jnp.where(names == features[MEMBER : MEMBER + 1, :], 1.0, 0.0).astype(BF16)
    scaled = field * area
    high = scaled.astype(BF16)
    low = (scaled - high.astype(F32)).astype(BF16)
    dims = (((1,), (1,)), ((), ()))
    return lax.dot_general(high, member, dims, preferred_element_type=F32) + lax.dot_general(
        low, member, dims, preferred_element_type=F32
    )


def self_body(
    rowblk, width, pair_ref, ltab_ref, rtab_ref, index_ref, count_ref, odd_ref, out_ref, live_ref,
    right_ref, left_ref, terms_ref, *slots
):
    _, rhs, panels = out_ref.shape
    groups, near = index_ref.shape
    turn = jnp.where(odd_ref[0] == 1, 0, 2 * panels)
    slot = lax.broadcasted_iota(jnp.int32, (1, near), 1)
    for group in range(groups):
        index = index_ref[group : group + 1, :]
        moved = jnp.where(index < panels, index + turn, index)
        index = jnp.where(index >= 2 * panels, index - turn, moved)
        live_ref[group : group + 1, :] = jnp.where(slot < count_ref[group], index, -LANES)
    write_terms(features_of(pair_ref[1]), terms_ref)
    right_ref[1] = right_side(terms_ref, rtab_ref[...])
    write_terms(features_of(pair_ref[0]), terms_ref)
    left_ref[...] = left_side(terms_ref, ltab_ref[...])
    right_ref[0] = right_side(terms_ref, rtab_ref[...])
    out_ref[...] = jnp.zeros_like(out_ref)

    def make(step, strip):
        start = pl.multiple_of(step * rowblk, rowblk)
        return tile_of(left_ref[pl.ds(start, rowblk), :], right_ref[0, :, strip : strip + width])

    def use(step, tile, strip, carry):
        if tile is None:
            return
        start = pl.multiple_of(step * rowblk, rowblk)
        out_ref[0, :, strip : strip + width] += jnp.dot(
            pair_ref[0, 0:rhs, pl.ds(start, rowblk)], tile, preferred_element_type=F32
        )

    two_stage(panels // rowblk, make, use, slots, width)


def self_field(pair, tables, index, count, odd):
    blocks, rows, panels = pair.shape
    rhs = rows - FEATURES
    rowblk, width = blocking(panels)
    vmem = pl.BlockSpec(memory_space=pltpu.VMEM)
    smem = pl.BlockSpec(memory_space=pltpu.SMEM)
    return pl.pallas_call(
        functools.partial(self_body, rowblk, width),
        out_shape=(
            jax.ShapeDtypeStruct((blocks, rhs, panels), F32),
            jax.ShapeDtypeStruct(index.shape, index.dtype),
            jax.ShapeDtypeStruct((blocks, DEPTH, panels), BF16),
        ),
        in_specs=[vmem] * 4 + [smem] * 2,
        out_specs=(vmem, vmem, vmem),
        scratch_shapes=[
            pltpu.VMEM((panels, DEPTH), BF16),
            pltpu.VMEM((TERMS, panels), F32),
            pltpu.VMEM((rowblk, panels), BF16),
            pltpu.VMEM((rowblk, panels), BF16),
        ],
        compiler_params=pltpu.CompilerParams(vmem_limit_bytes=VMEM_LIMIT),
        cost_estimate=pl.CostEstimate(flops=0, bytes_accessed=2**10, transcendentals=0),
    )(pair, *tables, index, count, odd)


def pairs_body(
    rowblk, width, pair_ref, far_ref, ltab_ref, right_ref, field_in, totals_in,
    field_ref, back_ref, totals_ref, left_ref, terms_ref, sum_ref, *slots
):
    blocks, rhs, panels = field_ref.shape
    for block in range(blocks):
        write_terms(features_of(far_ref[block]), terms_ref)
        left_ref[block] = left_side(terms_ref, ltab_ref[...])
    field_ref[...] = field_in[...]
    sum_ref[...] = jnp.zeros_like(sum_ref)
    chunks = panels // rowblk

    def place(step):
        turn = step // chunks
        start = pl.multiple_of((step % chunks) * rowblk, rowblk)
        return turn // blocks, turn % blocks, start

    def make(step, strip):
        far, own, start = place(step)
        return tile_of(
            left_ref[far, pl.ds(start, rowblk), :], right_ref[own, :, strip : strip + width]
        )

    def use(step, tile, strip, carry):
        far, own, start = place(step)
        if tile is None:
            sum_ref[far, :, pl.ds(start, rowblk)] += carry
            return
        part = lax.dot_general(
            pair_ref[own, 0:rhs, strip : strip + width], tile, (((1,), (1,)), ((), ())),
            preferred_element_type=F32,
        )
        field_ref[own, :, strip : strip + width] += jnp.dot(
            far_ref[far, 0:rhs, pl.ds(start, rowblk)], tile, preferred_element_type=F32
        )
        return part if carry is None else carry + part

    two_stage(blocks * blocks * chunks, make, use, slots, width)
    totals = totals_in[...]
    for block in range(blocks):
        totals = totals + totals_of(sum_ref[block], far_ref[block])
    totals_ref[...] = totals
    back_ref[...] = sum_ref[...].astype(BF16)


def pairs_field(pair, far, table, right, field, totals, last):
    blocks, rows, panels = pair.shape
    rhs = rows - FEATURES
    rowblk, width = blocking(panels)
    work = 3200 * panels * panels * blocks * blocks
    return in_vmem(
        functools.partial(pairs_body, rowblk, width),
        (
            jax.ShapeDtypeStruct((blocks, rhs, panels), F32),
            jax.ShapeDtypeStruct((blocks, rhs, panels), BF16),
            jax.ShapeDtypeStruct(totals.shape, F32),
        ),
        [
            pltpu.VMEM((blocks, panels, DEPTH), BF16),
            pltpu.VMEM((TERMS, panels), F32),
            pltpu.VMEM((blocks, rhs, panels), F32),
            pltpu.VMEM((rowblk, panels), BF16),
            pltpu.VMEM((rowblk, panels), BF16),
        ],
        flops=work if last else 0,
    )(pair, far, table, right, field, totals)


def near_body(
    together, twin_ref, own_ref, other_ref, index_ref, weight_ref, field_in, totals_in,
    pair_ref, field_ref, totals_ref, ext_ref
):
    rhs, panels = own_ref.shape
    groups, near = index_ref.shape
    pieces = panels // LANES
    for side, ref in enumerate((twin_ref, own_ref, other_ref)):
        for piece in range(pieces):
            start = rhs * (side * pieces + piece)
            ext_ref[start : start + rhs, :] = ref[:, piece * LANES : (piece + 1) * LANES]
    field_ref[...] = field_in[...]

    @pl.loop(0, groups // together)
    def _(batch):
        rows = [batch * together + member for member in range(together)]
        index = jnp.concatenate([index_ref[pl.ds(group, 1), :] for group in rows], axis=1)
        lane = index & (LANES - 1)
        place = jnp.broadcast_to(index >> (LANES.bit_length() - 1), (rhs, together * near))
        names = lax.broadcasted_iota(jnp.int32, (LANES, together * near), 0)
        pick = jnp.where(names == lane, 1.0, 0.0).astype(BF16)
        taken = jnp.zeros((rhs, together * near), F32)
        found = jnp.dot(ext_ref[...], pick, preferred_element_type=F32)
        for piece in range(3 * pieces):
            part = found[piece * rhs : (piece + 1) * rhs, :]
            taken = jnp.where(place == piece, part, taken)
        taken = taken.astype(BF16)
        width = weight_ref.shape[1]
        for member, group in enumerate(rows):
            field_ref[0, :, pl.ds(pl.multiple_of(group * width, width), width)] += lax.dot_general(
                taken[:, member * near : (member + 1) * near], weight_ref[group],
                (((1,), (1,)), ((), ())), preferred_element_type=F32,
            )

    totals = totals_in[...]
    for block in range(field_ref.shape[0]):
        totals = totals + totals_of(field_ref[block], pair_ref[block])
    height = totals_ref.shape[1]
    flat = jnp.concatenate([totals[r : r + height, :] for r in range(0, rhs, height)], axis=1)
    totals_ref[...] = jnp.broadcast_to(flat[None], totals_ref.shape)


def near_field(twin, own, other, index, weight, field, totals, pair):
    rhs, panels = own.shape
    vmem = pl.BlockSpec(memory_space=pltpu.VMEM)
    together = next(n for n in (4, 2, 1) if index.shape[0] % n == 0)
    return pl.pallas_call(
        functools.partial(near_body, together),
        out_shape=(
            jax.ShapeDtypeStruct(field.shape, F32),
            jax.ShapeDtypeStruct((lax.axis_size(AXES), rhs * rhs // 128, 128), F32),
        ),
        in_specs=[vmem] * 8,
        out_specs=(vmem, vmem),
        scratch_shapes=[pltpu.VMEM((3 * panels // LANES * rhs, LANES), BF16)],
        compiler_params=pltpu.CompilerParams(vmem_limit_bytes=VMEM_LIMIT),
        cost_estimate=pl.CostEstimate(flops=2 * 10**9, bytes_accessed=2**10, transcendentals=0),
    )(twin, own, other, index, weight, field, totals, pair)


def finish_body(field_ref, part_ref, totals_ref, potential_out, totals_out):
    potential_out[...] = field_ref[0] + part_ref[...].astype(F32)
    total = jnp.sum(totals_ref[...], axis=0)
    rhs, height = totals_out.shape[0], total.shape[0]
    for turn in range(rhs // height):
        totals_out[turn * height : (turn + 1) * height, :] = total[:, turn * rhs : (turn + 1) * rhs]


def send(value, source_of):
    count = lax.axis_size(AXES)
    return lax.ppermute(value, AXES, [(source_of(d), d) for d in range(count)])


def send_back(value, source_of):
    count = lax.axis_size(AXES)
    return lax.ppermute(value, AXES, [(d, source_of(d)) for d in range(count)])


def paired_blocks(geometry, charges, near_index, near_count, near_weight, conductor):
    cols = lax.axis_size("col")
    core, flip_x, far_z = cols, 2 * cols, cols // 2
    rhs = charges.shape[0]

    def partner(d, far):
        second = bool(d & core)
        mask = 1 + (flip_x if bool(d & 1) != second else 0) + (2 if second else 0)
        return d ^ (mask + (far_z if far else 0))

    def other_neighbour(d):
        count = lax.axis_size(AXES)
        return (d + (1 if d & 1 else -1)) % count

    tables = (chooser(True), chooser(False))
    bundle = make_bundle(geometry, charges, conductor)
    sibling = send(bundle, lambda d: d ^ core)
    pair = jnp.stack([bundle, sibling])
    close = send(pair, lambda d: partner(d, False))
    odd = (lax.axis_index(AXES) % 2).reshape(1)
    field, live, right = self_field(pair, tables, near_index, near_count, odd)
    late_pair, field = lax.optimization_barrier((pair, field))
    far = send(late_pair, lambda d: partner(d, True))
    totals = jnp.zeros((rhs, rhs), F32)
    field, close_back, totals = pairs_field(pair, close, tables[0], right, field, totals, False)
    close_back = send_back(close_back, lambda d: partner(d, False))
    late_charges, field = lax.optimization_barrier((charges, field))
    twin = send(late_charges, lambda d: d ^ 1)
    other = send(late_charges, other_neighbour)
    field, far_back, totals = pairs_field(pair, far, tables[0], right, field, totals, True)
    far_back = send_back(far_back, lambda d: partner(d, True))
    field, totals = near_field(
        twin, charges, other, live, near_weight, field, totals, pair
    )
    close_back, totals = lax.optimization_barrier((close_back, totals))
    totals = lax.all_to_all(totals, AXES, 0, 0, tiled=True)
    field = field + close_back.astype(F32) + far_back.astype(F32)
    twin_part = send(field[1].astype(BF16), lambda d: d ^ core)
    return in_vmem(
        finish_body,
        (jax.ShapeDtypeStruct(charges.shape, F32), jax.ShapeDtypeStruct((rhs, rhs), F32)),
    )(field, twin_part, totals)


def passed_along(value, axis, steps):
    count = lax.axis_size(axis)
    pairs = [(source, (source + steps) % count) for source in range(count)]
    return lax.ppermute(value, axis, pairs)


def extended_2(x, sides, width):
    for axis, dim in sides:
        count, length = (lax.axis_size(axis), x.shape[dim])
        up = [(i, (i + 1) % count) for i in range(count)]
        down = [(j, i) for i, j in up]
        last = lax.slice_in_dim(x, length - width, length, axis=dim)
        initial = lax.slice_in_dim(x, 0, width, axis=dim)
        before = lax.ppermute(last, axis, up)
        after = lax.ppermute(initial, axis, down)
        x = jnp.concatenate([before, x, after], axis=dim)
    return x


def kernel_tile(rows, cols):
    delta_x = rows[0][:, None] - cols[0][None, :]
    delta_y = rows[1][:, None] - cols[1][None, :]
    delta_z = rows[2][:, None] - cols[2][None, :]
    spread = rows[3][:, None] * rows[3][:, None] + cols[3][None, :] * cols[3][None, :]
    squared = delta_x * delta_x + delta_y * delta_y + delta_z * delta_z + spread
    return lax.rsqrt(squared).astype(BF16)


def pair_products(own_geo, own_w, other_geo, other_w, backwards):
    panels = own_geo.shape[1]
    rowblk = min(256, panels)
    pieces = []
    back = jnp.zeros(other_w.shape, F32)
    for start in range(0, panels, rowblk):
        tile = kernel_tile(own_geo[:, start : start + rowblk], other_geo)
        pieces.append(
            lax.dot_general(
                other_w, tile, (((1,), (1,)), ((), ())), preferred_element_type=F32
            )
        )
        if backwards:
            back = back + jnp.dot(
                own_w[:, start : start + rowblk], tile, preferred_element_type=F32
            )
    return (jnp.concatenate(pieces, axis=1), back)


def from_lower(geometry, weighted, offset):
    geo = passed_along(geometry, ("row", "col"), offset)
    wts = passed_along(weighted, ("row", "col"), offset)
    return (geo, wts)


def give_back(partial_value, offset):
    return passed_along(partial_value, ("row", "col"), -offset)


def offset_rounds(geometry, charges, near_index, near_count, near_weight, conductor):
    devices = lax.axis_size(("row", "col"))
    stride = devices // (2 * ROUNDS)
    offsets = [1 + k * stride for k in range(ROUNDS)]
    panels = charges.shape[1]
    groups_dev = near_index.shape[0]
    area = geometry[3] * geometry[3]
    weighted = (charges.astype(F32) * area[None, :]).astype(BF16)
    field, unused = pair_products(geometry, weighted, geometry, weighted, False)
    for turn in range(ROUNDS):
        offset = offsets[turn]
        lower_geo, lower_w = from_lower(geometry, weighted, offset)
        forward, back = pair_products(geometry, weighted, lower_geo, lower_w, True)
        field = field + forward + give_back(back.astype(BF16), offset).astype(F32)
    extended = extended_2(charges, ((("row", "col"), 1),), panels)
    gathered = jnp.take(extended, near_index.reshape(-1), axis=1).reshape(
        charges.shape[0], groups_dev, near_index.shape[1]
    )
    live = jnp.arange(near_index.shape[1], dtype=jnp.int32)[None, :] < near_count[:, None]
    gathered = jnp.where(live[None], gathered, jnp.zeros_like(gathered))
    correction = jnp.einsum(
        "rgk,gtk->rgt", gathered, near_weight, preferred_element_type=F32
    )
    field = field + correction.reshape(charges.shape[0], panels)
    member = (conductor[:, None] == jnp.arange(charges.shape[0], dtype=jnp.int32)[None, :]).astype(
        F32
    )
    local_totals = jnp.dot(
        field * area[None, :],
        member,
        precision=lax.Precision.HIGHEST,
        preferred_element_type=F32,
    )
    totals = lax.psum(local_totals, ("row", "col"))
    return (field, totals)


def on_device(geometry, *rest):
    if lax.axis_size(AXES) == 4 * ROUNDS:
        return paired_blocks(geometry, *rest)
    return offset_rounds(geometry, *rest)


def solution(mesh):
    in_specs = (
        P(None, ("row", "col")),
        P(None, ("row", "col")),
        P(("row", "col"), None),
        P(("row", "col")),
        P(("row", "col"), None, None),
        P(("row", "col")),
    )
    out_specs = (P(None, ("row", "col")), P())
    return jax.shard_map(
        on_device, mesh=mesh, in_specs=in_specs, out_specs=out_specs, check_vma=False
    )
```

```python
import functools

import jax
import jax.numpy as jnp
import numpy as np
from jax import lax
from jax.experimental import pallas as pl
from jax.experimental.pallas import tpu as pltpu
from jax.sharding import PartitionSpec as P

ROUNDS = 8
AXES = ("row", "col")
F32 = jnp.float32
BF16 = jnp.bfloat16

X, AREA, MEMBER = 0, 6, 7
FEATURES = 8
NORM, ONE = 8, 11
TERMS = 16
LANES = 128
DEPTH = 32
VMEM_LIMIT = 48 * 2**20


def chooser(left):
    table = np.zeros((DEPTH, TERMS), np.float32)
    row = 0
    for axis in range(3):
        for first in range(2):
            for second in range(2):
                feature = X + 2 * axis + (first if left else second)
                table[row, feature] = 1.0 if left else -2.0
                row += 1
    for term in range(3):
        table[row, NORM + term if left else ONE] = 1.0
        table[row + 3, ONE if left else NORM + term] = 1.0
        row += 1
    return jnp.asarray(table, BF16)


def blocking(panels):
    rows = next((r for r in (384, 256, 128) if panels % (2 * r) == 0), panels // 2)
    return rows, 256 if panels % 256 == 0 else panels


def in_vmem(body, out_shape, scratch=(), flops=0):
    return pl.pallas_call(
        body,
        out_shape=out_shape,
        scratch_shapes=list(scratch),
        compiler_params=pltpu.CompilerParams(vmem_limit_bytes=VMEM_LIMIT),
        cost_estimate=pl.CostEstimate(flops=flops, bytes_accessed=2**10, transcendentals=0),
    )


def rounded(value):
    return value.astype(BF16).astype(F32)


def bundle_body(geo_ref, charges_ref, conductor_ref, out_ref, rows_ref):
    rhs = charges_ref.shape[0]
    size = geo_ref[3:4, :]
    area = size * size
    rows_ref[0:rhs, :] = charges_ref[...].astype(F32) * area
    for axis in range(3):
        value = geo_ref[axis : axis + 1, :]
        high = rounded(value)
        row = rhs + X + 2 * axis
        rows_ref[row : row + 1, :] = high
        rows_ref[row + 1 : row + 2, :] = value - high
    rows_ref[rhs + AREA : rhs + AREA + 1, :] = area
    rows_ref[rhs + MEMBER : rhs + MEMBER + 1, :] = conductor_ref[...].astype(F32).reshape(1, -1)
    out_ref[...] = rows_ref[...].astype(BF16)


def features_of(bundle):
    rows = bundle.shape[0]
    return bundle.astype(F32)[rows - FEATURES :, :]


def write_terms(features, terms_ref):
    norm = features[AREA : AREA + 1, :]
    for axis in range(3):
        row = X + 2 * axis
        kept = features[row : row + 1, :] + features[row + 1 : row + 2, :]
        norm = norm + kept * kept
    terms_ref[0:FEATURES, :] = features
    terms_ref[NORM:, :] = jnp.zeros((TERMS - NORM, norm.shape[1]), F32)
    for term in range(3):
        part = rounded(norm)
        terms_ref[NORM + term : NORM + term + 1, :] = part
        norm = norm - part
    terms_ref[ONE : ONE + 1, :] = jnp.ones_like(norm)


def make_bundle(geometry, charges, conductor):
    rhs, panels = charges.shape
    return in_vmem(
        bundle_body,
        jax.ShapeDtypeStruct((rhs + FEATURES, panels), BF16),
        [pltpu.VMEM((rhs + FEATURES, panels), F32)],
    )(geometry, charges, conductor)


def left_side(terms_ref, table):
    return lax.dot_general(
        terms_ref[...].astype(BF16), table, (((0,), (1,)), ((), ())), preferred_element_type=F32
    ).astype(BF16)


def right_side(terms_ref, table):
    return jnp.dot(table, terms_ref[...].astype(BF16), preferred_element_type=F32).astype(BF16)


def tile_of(left, right):
    return lax.rsqrt(jnp.dot(left, right, preferred_element_type=F32)).astype(BF16)


def two_stage(steps, make, use, slots, width):
    strips = range(0, slots[0].shape[1], width)

    def one(step, now, later):
        carry = None
        for start in strips:
            if later is not None:
                later[:, start : start + width] = make(step + 1, start)
            carry = use(step, now[:, start : start + width], start, carry)
        use(step, None, None, carry)

    for start in strips:
        slots[0][:, start : start + width] = make(0, start)

    @pl.loop(0, steps // 2 - 1)
    def _(half):
        one(2 * half, slots[0], slots[1])
        one(2 * half + 1, slots[1], slots[0])

    one(steps - 2, slots[0], slots[1])
    one(steps - 1, slots[1], None)


def totals_of(field, bundle):
    rhs = field.shape[0]
    features = features_of(bundle)
    area = features[AREA : AREA + 1, :]
    names = lax.broadcasted_iota(jnp.int32, field.shape, 0).astype(F32)
    member = jnp.where(names == features[MEMBER : MEMBER + 1, :], 1.0, 0.0).astype(BF16)
    scaled = field * area
    high = scaled.astype(BF16)
    low = (scaled - high.astype(F32)).astype(BF16)
    dims = (((1,), (1,)), ((), ()))
    return lax.dot_general(high, member, dims, preferred_element_type=F32) + lax.dot_general(
        low, member, dims, preferred_element_type=F32
    )


def self_body(
    rowblk, width, pair_ref, ltab_ref, rtab_ref, index_ref, count_ref, odd_ref, out_ref, live_ref,
    right_ref, left_ref, terms_ref, *slots
):
    _, rhs, panels = out_ref.shape
    groups, near = index_ref.shape
    turn = jnp.where(odd_ref[0] == 1, 0, 2 * panels)
    slot = lax.broadcasted_iota(jnp.int32, (1, near), 1)
    for group in range(groups):
        index = index_ref[group : group + 1, :]
        moved = jnp.where(index < panels, index + turn, index)
        index = jnp.where(index >= 2 * panels, index - turn, moved)
        live_ref[group : group + 1, :] = jnp.where(slot < count_ref[group], index, -LANES)
    write_terms(features_of(pair_ref[1]), terms_ref)
    right_ref[1] = right_side(terms_ref, rtab_ref[...])
    write_terms(features_of(pair_ref[0]), terms_ref)
    left_ref[...] = left_side(terms_ref, ltab_ref[...])
    right_ref[0] = right_side(terms_ref, rtab_ref[...])
    out_ref[...] = jnp.zeros_like(out_ref)

    def make(step, strip):
        start = pl.multiple_of(step * rowblk, rowblk)
        return tile_of(left_ref[pl.ds(start, rowblk), :], right_ref[0, :, strip : strip + width])

    def use(step, tile, strip, carry):
        if tile is None:
            return
        start = pl.multiple_of(step * rowblk, rowblk)
        out_ref[0, :, strip : strip + width] += jnp.dot(
            pair_ref[0, 0:rhs, pl.ds(start, rowblk)], tile, preferred_element_type=F32
        )

    two_stage(panels // rowblk, make, use, slots, width)


def self_field(pair, tables, index, count, odd):
    blocks, rows, panels = pair.shape
    rhs = rows - FEATURES
    rowblk, width = blocking(panels)
    vmem = pl.BlockSpec(memory_space=pltpu.VMEM)
    smem = pl.BlockSpec(memory_space=pltpu.SMEM)
    return pl.pallas_call(
        functools.partial(self_body, rowblk, width),
        out_shape=(
            jax.ShapeDtypeStruct((blocks, rhs, panels), F32),
            jax.ShapeDtypeStruct(index.shape, index.dtype),
            jax.ShapeDtypeStruct((blocks, DEPTH, panels), BF16),
        ),
        in_specs=[vmem] * 4 + [smem] * 2,
        out_specs=(vmem, vmem, vmem),
        scratch_shapes=[
            pltpu.VMEM((panels, DEPTH), BF16),
            pltpu.VMEM((TERMS, panels), F32),
            pltpu.VMEM((rowblk, panels), BF16),
            pltpu.VMEM((rowblk, panels), BF16),
        ],
        compiler_params=pltpu.CompilerParams(vmem_limit_bytes=VMEM_LIMIT),
        cost_estimate=pl.CostEstimate(flops=0, bytes_accessed=2**10, transcendentals=0),
    )(pair, *tables, index, count, odd)


def pairs_body(
    rowblk, width, pair_ref, far_ref, ltab_ref, right_ref, field_in, totals_in,
    field_ref, back_ref, totals_ref, left_ref, terms_ref, sum_ref, *slots
):
    blocks, rhs, panels = field_ref.shape
    for block in range(blocks):
        write_terms(features_of(far_ref[block]), terms_ref)
        left_ref[block] = left_side(terms_ref, ltab_ref[...])
    field_ref[...] = field_in[...]
    sum_ref[...] = jnp.zeros_like(sum_ref)
    chunks = panels // rowblk

    def place(step):
        turn = step // chunks
        start = pl.multiple_of((step % chunks) * rowblk, rowblk)
        return turn // blocks, turn % blocks, start

    def make(step, strip):
        far, own, start = place(step)
        return tile_of(
            left_ref[far, pl.ds(start, rowblk), :], right_ref[own, :, strip : strip + width]
        )

    def use(step, tile, strip, carry):
        far, own, start = place(step)
        if tile is None:
            sum_ref[far, :, pl.ds(start, rowblk)] += carry
            return
        part = lax.dot_general(
            pair_ref[own, 0:rhs, strip : strip + width], tile, (((1,), (1,)), ((), ())),
            preferred_element_type=F32,
        )
        field_ref[own, :, strip : strip + width] += jnp.dot(
            far_ref[far, 0:rhs, pl.ds(start, rowblk)], tile, preferred_element_type=F32
        )
        return part if carry is None else carry + part

    two_stage(blocks * blocks * chunks, make, use, slots, width)
    totals = totals_in[...]
    for block in range(blocks):
        totals = totals + totals_of(sum_ref[block], far_ref[block])
    totals_ref[...] = totals
    back_ref[...] = sum_ref[...].astype(BF16)


def pairs_field(pair, far, table, right, field, totals, last):
    blocks, rows, panels = pair.shape
    rhs = rows - FEATURES
    rowblk, width = blocking(panels)
    work = 3200 * panels * panels * blocks * blocks
    return in_vmem(
        functools.partial(pairs_body, rowblk, width),
        (
            jax.ShapeDtypeStruct((blocks, rhs, panels), F32),
            jax.ShapeDtypeStruct((blocks, rhs, panels), BF16),
            jax.ShapeDtypeStruct(totals.shape, F32),
        ),
        [
            pltpu.VMEM((blocks, panels, DEPTH), BF16),
            pltpu.VMEM((TERMS, panels), F32),
            pltpu.VMEM((blocks, rhs, panels), F32),
            pltpu.VMEM((rowblk, panels), BF16),
            pltpu.VMEM((rowblk, panels), BF16),
        ],
        flops=work if last else 0,
    )(pair, far, table, right, field, totals)


def near_body(
    together, twin_ref, own_ref, other_ref, index_ref, weight_ref, field_in, totals_in,
    pair_ref, field_ref, totals_ref, ext_ref
):
    rhs, panels = own_ref.shape
    groups, near = index_ref.shape
    pieces = panels // LANES
    for side, ref in enumerate((twin_ref, own_ref, other_ref)):
        for piece in range(pieces):
            start = rhs * (side * pieces + piece)
            ext_ref[start : start + rhs, :] = ref[:, piece * LANES : (piece + 1) * LANES]
    field_ref[...] = field_in[...]

    @pl.loop(0, groups // together)
    def _(batch):
        rows = [batch * together + member for member in range(together)]
        index = jnp.concatenate([index_ref[pl.ds(group, 1), :] for group in rows], axis=1)
        lane = index & (LANES - 1)
        place = jnp.broadcast_to(index >> (LANES.bit_length() - 1), (rhs, together * near))
        names = lax.broadcasted_iota(jnp.int32, (LANES, together * near), 0)
        pick = jnp.where(names == lane, 1.0, 0.0).astype(BF16)
        taken = jnp.zeros((rhs, together * near), F32)
        found = jnp.dot(ext_ref[...], pick, preferred_element_type=F32)
        for piece in range(3 * pieces):
            part = found[piece * rhs : (piece + 1) * rhs, :]
            taken = jnp.where(place == piece, part, taken)
        taken = taken.astype(BF16)
        width = weight_ref.shape[1]
        for member, group in enumerate(rows):
            field_ref[0, :, pl.ds(pl.multiple_of(group * width, width), width)] += lax.dot_general(
                taken[:, member * near : (member + 1) * near], weight_ref[group],
                (((1,), (1,)), ((), ())), preferred_element_type=F32,
            )

    totals = totals_in[...]
    for block in range(field_ref.shape[0]):
        totals = totals + totals_of(field_ref[block], pair_ref[block])
    height = totals_ref.shape[1]
    flat = jnp.concatenate([totals[r : r + height, :] for r in range(0, rhs, height)], axis=1)
    totals_ref[...] = jnp.broadcast_to(flat[None], totals_ref.shape)


def near_field(twin, own, other, index, weight, field, totals, pair):
    rhs, panels = own.shape
    vmem = pl.BlockSpec(memory_space=pltpu.VMEM)
    together = next(n for n in (4, 2, 1) if index.shape[0] % n == 0)
    return pl.pallas_call(
        functools.partial(near_body, together),
        out_shape=(
            jax.ShapeDtypeStruct(field.shape, F32),
            jax.ShapeDtypeStruct((lax.axis_size(AXES), rhs * rhs // 128, 128), F32),
        ),
        in_specs=[vmem] * 8,
        out_specs=(vmem, vmem),
        scratch_shapes=[pltpu.VMEM((3 * panels // LANES * rhs, LANES), BF16)],
        compiler_params=pltpu.CompilerParams(vmem_limit_bytes=VMEM_LIMIT),
        cost_estimate=pl.CostEstimate(flops=2 * 10**9, bytes_accessed=2**10, transcendentals=0),
    )(twin, own, other, index, weight, field, totals, pair)


def finish_body(field_ref, part_ref, totals_ref, potential_out, totals_out):
    potential_out[...] = field_ref[0] + part_ref[...].astype(F32)
    total = jnp.sum(totals_ref[...], axis=0)
    rhs, height = totals_out.shape[0], total.shape[0]
    for turn in range(rhs // height):
        totals_out[turn * height : (turn + 1) * height, :] = total[:, turn * rhs : (turn + 1) * rhs]


def send(value, source_of):
    count = lax.axis_size(AXES)
    return lax.ppermute(value, AXES, [(source_of(d), d) for d in range(count)])


def send_back(value, source_of):
    count = lax.axis_size(AXES)
    return lax.ppermute(value, AXES, [(d, source_of(d)) for d in range(count)])


def paired_blocks(geometry, charges, near_index, near_count, near_weight, conductor):
    cols = lax.axis_size("col")
    core, flip_x, far_z = cols, 2 * cols, cols // 2
    rhs = charges.shape[0]

    def partner(d, far):
        second = bool(d & core)
        mask = 1 + (flip_x if bool(d & 1) != second else 0) + (2 if second else 0)
        return d ^ (mask + (far_z if far else 0))

    def other_neighbour(d):
        count = lax.axis_size(AXES)
        return (d + (1 if d & 1 else -1)) % count

    tables = (chooser(True), chooser(False))
    bundle = make_bundle(geometry, charges, conductor)
    sibling = send(bundle, lambda d: d ^ core)
    pair = jnp.stack([bundle, sibling])
    close = send(pair, lambda d: partner(d, False))
    odd = (lax.axis_index(AXES) % 2).reshape(1)
    field, live, right = self_field(pair, tables, near_index, near_count, odd)
    late_pair, field = lax.optimization_barrier((pair, field))
    far = send(late_pair, lambda d: partner(d, True))
    totals = jnp.zeros((rhs, rhs), F32)
    late_charges, close = lax.optimization_barrier((charges, close))
    twin = send(late_charges, lambda d: d ^ 1)
    other = send(late_charges, other_neighbour)
    field, close_back, totals = pairs_field(pair, close, tables[0], right, field, totals, False)
    close_back = send_back(close_back, lambda d: partner(d, False))
    field, far_back, totals = pairs_field(pair, far, tables[0], right, field, totals, True)
    far_back = send_back(far_back, lambda d: partner(d, True))
    field, totals = near_field(
        twin, charges, other, live, near_weight, field, totals, pair
    )
    close_back, totals = lax.optimization_barrier((close_back, totals))
    totals = lax.all_to_all(totals, AXES, 0, 0, tiled=True)
    field = field + close_back.astype(F32) + far_back.astype(F32)
    twin_part = send(field[1].astype(BF16), lambda d: d ^ core)
    return in_vmem(
        finish_body,
        (jax.ShapeDtypeStruct(charges.shape, F32), jax.ShapeDtypeStruct((rhs, rhs), F32)),
    )(field, twin_part, totals)


def passed_along(value, axis, steps):
    count = lax.axis_size(axis)
    pairs = [(source, (source + steps) % count) for source in range(count)]
    return lax.ppermute(value, axis, pairs)


def extended_2(x, sides, width):
    for axis, dim in sides:
        count, length = (lax.axis_size(axis), x.shape[dim])
        up = [(i, (i + 1) % count) for i in range(count)]
        down = [(j, i) for i, j in up]
        last = lax.slice_in_dim(x, length - width, length, axis=dim)
        initial = lax.slice_in_dim(x, 0, width, axis=dim)
        before = lax.ppermute(last, axis, up)
        after = lax.ppermute(initial, axis, down)
        x = jnp.concatenate([before, x, after], axis=dim)
    return x


def kernel_tile(rows, cols):
    delta_x = rows[0][:, None] - cols[0][None, :]
    delta_y = rows[1][:, None] - cols[1][None, :]
    delta_z = rows[2][:, None] - cols[2][None, :]
    spread = rows[3][:, None] * rows[3][:, None] + cols[3][None, :] * cols[3][None, :]
    squared = delta_x * delta_x + delta_y * delta_y + delta_z * delta_z + spread
    return lax.rsqrt(squared).astype(BF16)


def pair_products(own_geo, own_w, other_geo, other_w, backwards):
    panels = own_geo.shape[1]
    rowblk = min(256, panels)
    pieces = []
    back = jnp.zeros(other_w.shape, F32)
    for start in range(0, panels, rowblk):
        tile = kernel_tile(own_geo[:, start : start + rowblk], other_geo)
        pieces.append(
            lax.dot_general(
                other_w, tile, (((1,), (1,)), ((), ())), preferred_element_type=F32
            )
        )
        if backwards:
            back = back + jnp.dot(
                own_w[:, start : start + rowblk], tile, preferred_element_type=F32
            )
    return (jnp.concatenate(pieces, axis=1), back)


def from_lower(geometry, weighted, offset):
    geo = passed_along(geometry, ("row", "col"), offset)
    wts = passed_along(weighted, ("row", "col"), offset)
    return (geo, wts)


def give_back(partial_value, offset):
    return passed_along(partial_value, ("row", "col"), -offset)


def offset_rounds(geometry, charges, near_index, near_count, near_weight, conductor):
    devices = lax.axis_size(("row", "col"))
    stride = devices // (2 * ROUNDS)
    offsets = [1 + k * stride for k in range(ROUNDS)]
    panels = charges.shape[1]
    groups_dev = near_index.shape[0]
    area = geometry[3] * geometry[3]
    weighted = (charges.astype(F32) * area[None, :]).astype(BF16)
    field, unused = pair_products(geometry, weighted, geometry, weighted, False)
    for turn in range(ROUNDS):
        offset = offsets[turn]
        lower_geo, lower_w = from_lower(geometry, weighted, offset)
        forward, back = pair_products(geometry, weighted, lower_geo, lower_w, True)
        field = field + forward + give_back(back.astype(BF16), offset).astype(F32)
    extended = extended_2(charges, ((("row", "col"), 1),), panels)
    gathered = jnp.take(extended, near_index.reshape(-1), axis=1).reshape(
        charges.shape[0], groups_dev, near_index.shape[1]
    )
    live = jnp.arange(near_index.shape[1], dtype=jnp.int32)[None, :] < near_count[:, None]
    gathered = jnp.where(live[None], gathered, jnp.zeros_like(gathered))
    correction = jnp.einsum(
        "rgk,gtk->rgt", gathered, near_weight, preferred_element_type=F32
    )
    field = field + correction.reshape(charges.shape[0], panels)
    member = (conductor[:, None] == jnp.arange(charges.shape[0], dtype=jnp.int32)[None, :]).astype(
        F32
    )
    local_totals = jnp.dot(
        field * area[None, :],
        member,
        precision=lax.Precision.HIGHEST,
        preferred_element_type=F32,
    )
    totals = lax.psum(local_totals, ("row", "col"))
    return (field, totals)


def on_device(geometry, *rest):
    if lax.axis_size(AXES) == 4 * ROUNDS:
        return paired_blocks(geometry, *rest)
    return offset_rounds(geometry, *rest)


def solution(mesh):
    in_specs = (
        P(None, ("row", "col")),
        P(None, ("row", "col")),
        P(("row", "col"), None),
        P(("row", "col")),
        P(("row", "col"), None, None),
        P(("row", "col")),
    )
    out_specs = (P(None, ("row", "col")), P())
    return jax.shard_map(
        on_device, mesh=mesh, in_specs=in_specs, out_specs=out_specs, check_vma=False
    )
```
